512 devices in a mesh: pb: 32 (over y, x), row: 16 (over z, core).
Axes of the slice: x: 4, y: 8, z: 8, core: 2. Of those that a mesh axis runs over, the one named last changes fastest.
Arguments:
- valence_bands: bfloat16 [32, 20, 4096], P('pb', None, 'row'), may hold values from -0.75 to 0.75
- conduction_bands: bfloat16 [32, 20, 4096], P('pb', None, 'row'), may hold values from -6 to 6
- screened: bfloat16 [32, 4096, 4096], P('pb', 'row'), may hold values from -0.09375 to 0.09375
- pair_list: int32 [64, 2], replicated, may hold values from 0 to 31, as said below
- transfer_index: int32 [64, 1], replicated, may hold values from 0 to 31; in each aligned block of 64 rows (0 to 63, 64 to 127, ...) at most 6 rows name the same one
- owner_map: int32 [32], replicated, may hold values from 0 to 31, as said below
Outputs:
- direct: bfloat16 [64, 400, 400], P('pb', 'row')
- mirror: bfloat16 [64, 400, 400], P('pb', 'row')
The draws below stay inside these ranges and needn't reach their ends.
Inputs may be any that keep to these rules, and one draw needn't show every extreme that they name: owner_map is a permutation of 0 to 31. `pair_list`: the two k-points of a pair differ. The first k-point of pairs e * 2 to e * 2 + 1 is the one that owner_map sends to e. Over all pairs, the second k-points are sent by owner_map to every value 0 to 31 exactly 2 times. `transfer_index`: at most 6 pairs share one momentum transfer, and some transfer has exactly 6; every transfer has at least one pair.
All inputs are finite; a program needn't handle non-finite values.
Results may differ from the reference program's by a relative error of at most 0.0065.
Values may be sent and summed in bfloat16 or wider, within the bound.
A program may use at most 64 MiB of HBM per device.

```python
import math
import jax
import jax.numpy as jnp
import numpy as np
from jax import lax

NMU = 4096
NV = 20
NC = 20
PAIR_DEV = 2
MOST = 6
NK = 32
NQ = 32
NPAIRS = 64
N_PB = 32


def pair_layout(key):
    owner_map = jax.random.permutation(jax.random.fold_in(key, 71), NK).astype(jnp.int32)
    holder = jnp.argsort(owner_map).astype(jnp.int32)
    columns = []
    for repeat in range(PAIR_DEV):
        shuffle = jax.random.permutation(jax.random.fold_in(key, 100 + repeat), NK).astype(jnp.int32)
        inverse = jnp.argsort(shuffle).astype(jnp.int32)
        offset = jax.random.randint(jax.random.fold_in(key, 300 + repeat), (), 1, NK).astype(jnp.int32)
        partner = inverse[(shuffle + offset) % NK]
        columns.append(jnp.stack([holder, holder[partner]], axis=1))
    pair_list = jnp.stack(columns, axis=1).reshape(NK * PAIR_DEV, 2).astype(jnp.int32)
    return (owner_map, pair_list)


def draw_pair_list(key, part):
    return pair_layout(key)[1]


def draw_owner_map(key, part):
    return pair_layout(key)[0]


def shard_levels(rng, shape, shards, smallest, largest):
    def one(axis_at, shards_of):
        heights = jax.random.uniform(jax.random.fold_in(jax.random.fold_in(rng, 6), axis_at), (shards_of,), jnp.float32, smallest / len(shards), largest / len(shards))
        return jnp.repeat(jnp.exp(heights), shape[axis_at] // shards_of).reshape((-1,) + (1,) * (len(shape) - axis_at - 1))

    gain = one(*shards[0])
    for cut in shards[1:]:
        gain = gain * one(*cut)
    return gain


def deal_out(stream_key, own, number, rows, amount, top, most, slope):
    sequence = jax.random.permutation(stream_key, amount)
    heavy_load, ordinary = shares(amount, rows * top, most, slope, True), shares(amount, rows * top, most, slope, False)
    places = jnp.arange(amount)

    def named(sizes, offset_by):
        used = int((sizes > 0).sum())
        fixed = max(1, used // 4)
        moved = fixed + (places - fixed + offset_by * (used - fixed)) % max(1, amount - fixed)
        return jnp.zeros((amount,), jnp.int32).at[sequence[jnp.where(places < fixed, places, moved)]].set(jnp.asarray(sizes, jnp.int32))

    sizes = jnp.where(number % 4 == 0, named(heavy_load, number // 4), named(ordinary, number - number // 4 - 1))
    mixed = jax.random.permutation(jax.random.fold_in(own, 3), amount)
    giver, receiver = mixed[0:amount // 2 * 2:2], mixed[1:amount // 2 * 2:2]
    slack = jnp.minimum(sizes[giver] - 1, most - sizes[receiver]) // 2
    slack = jnp.where((giver == sequence[0]) | (receiver == sequence[0]) | (sizes[receiver] == 0), 0, jnp.maximum(slack, 0))
    moved = jax.random.randint(jax.random.fold_in(own, 4), (amount // 2,), 0, 1 << 20) % (slack + 1)
    sizes = sizes.at[giver].add(-moved).at[receiver].add(moved)
    members = jnp.searchsorted(jnp.cumsum(sizes), jnp.arange(rows * top), side="right").astype(jnp.int32)
    table = members.reshape(top, rows).T
    table = table[jax.random.permutation(jax.random.fold_in(own, 1), rows)]
    offset_by = jax.random.randint(jax.random.fold_in(own, 2), (rows, 1), 0, top)
    return jnp.take_along_axis(table, (jnp.arange(top)[None, :] + offset_by) % top, axis=1)


def shares(number_of, total, limit, skew, full):
    portions = [(1 << 20) // math.isqrt(standing ** skew) + 1 for standing in range(1, number_of + 1)]
    largest = limit if full else min(limit, max(-(-total // number_of), total * portions[0] // sum(portions)))
    least = 1 if total - largest >= number_of - 1 else 0
    counts, rest = [largest] + [least] * (number_of - 1), total - largest - least * (number_of - 1)
    while rest > 0:
        free = [i for i in range(1, number_of) if counts[i] < largest] or [i for i in range(1, number_of) if counts[i] < limit]
        mass, left = sum([portions[i] for i in free]), rest
        for i in free:
            extra = min(limit - counts[i], max(1, left * portions[i] // mass), rest)
            counts[i] = counts[i] + extra
            rest = rest - extra
    return np.array(counts)


def gaussian(key, dims, width, most, cuts=(), kind=jnp.bfloat16):
    result = width * jax.random.normal(key, dims, jnp.float32)
    if cuts:
        result = result * shard_levels(key, dims, cuts, -0.22, 0.18)
    return jnp.clip(result, -most, most).astype(kind)


def setup_inputs(seed: int = 0) -> dict:
    key_of = jax.random.split(jax.random.key(seed), 7)
    valence_bands = gaussian(key_of[0], (NK, NV, NMU), 0.125, 0.75, ((0, 32), (2, 16)))
    conduction_bands = gaussian(key_of[1], (NK, NC, NMU), 1.0, 6.0, ((0, 32), (2, 16)))
    screened = gaussian(key_of[2], (NQ, NMU, NMU), NMU ** -0.5, 0.09375, ((0, 32), (1, 16)))
    pair_list = draw_pair_list(jax.random.fold_in(key_of[6], 71), 0)
    transfer_index_keys = jax.random.split(jax.random.fold_in(key_of[4], 1), NPAIRS // NPAIRS)
    transfer_index_turns = jax.random.permutation(jax.random.fold_in(key_of[4], 3), NPAIRS // NPAIRS)
    transfer_index = jax.vmap(lambda own, number: deal_out(jax.random.fold_in(key_of[4], 2), own, number, NPAIRS, NQ, 1, MOST, 2))(transfer_index_keys, transfer_index_turns).reshape((NPAIRS, 1))
    owner_map = draw_owner_map(jax.random.fold_in(key_of[6], 71), 0)
    return dict(valence_bands=valence_bands, conduction_bands=conduction_bands, screened=screened, pair_list=pair_list, transfer_index=transfer_index, owner_map=owner_map)


def rank_table(labels, groups, slots_per):
    total_rows = labels.shape[0]
    member = (labels[None, :] == jnp.arange(groups, dtype=jnp.int32)[:, None]).astype(jnp.int32)
    before = jnp.cumsum(member, axis=1) - 1
    placed = member[:, None, :] * (before[:, None, :] == jnp.arange(slots_per, dtype=jnp.int32)[None, :, None]).astype(jnp.int32)
    numbers = jnp.arange(total_rows, dtype=jnp.int32) + 1
    return (jnp.sum(placed * numbers[None, None, :], axis=2) - 1).astype(jnp.int32)


def pair_kernel(val_first, val_second, con_first, con_second, screen_rows):
    val_count = val_first.shape[0]
    con_count = con_first.shape[0]
    val_pairs = (val_first[:, None, :].astype(jnp.float32) * val_second[None, :, :].astype(jnp.float32))
    val_pairs = val_pairs.reshape(val_count * val_count, val_first.shape[1]).astype(jnp.bfloat16)
    con_pairs = (con_first[:, None, :].astype(jnp.float32) * con_second[None, :, :].astype(jnp.float32))
    con_pairs = con_pairs.reshape(con_count * con_count, con_first.shape[1]).astype(jnp.bfloat16)
    interim = lax.dot_general(screen_rows, con_pairs, (((1,), (1,)), ((), ())), preferred_element_type=jnp.float32).astype(jnp.bfloat16)
    partial_sum = jnp.dot(val_pairs, interim, preferred_element_type=jnp.float32)
    partial_sum = partial_sum.reshape(val_count, val_count, con_count, con_count).transpose(0, 2, 1, 3)
    return partial_sum.reshape(val_count * con_count, val_count * con_count)


def reference(valence_bands, conduction_bands, screened, pair_list, transfer_index, owner_map):
    slot_first = jnp.take(owner_map, pair_list[:, 0]).astype(jnp.int32)
    slot_second = jnp.take(owner_map, pair_list[:, 1]).astype(jnp.int32)
    transfers = transfer_index[:, 0].astype(jnp.int32)

    def one_pair(operands):
        first_slot, second_slot, which = operands
        block = pair_kernel(valence_bands[first_slot], valence_bands[second_slot], conduction_bands[first_slot], conduction_bands[second_slot], screened[which])
        return block.astype(jnp.bfloat16)

    direct = lax.map(one_pair, (slot_first, slot_second, transfers))
    mirror_order = rank_table(slot_second, N_PB, PAIR_DEV).reshape(-1)
    mirror = jnp.transpose(jnp.take(direct, mirror_order, axis=0), (0, 2, 1))
    return direct, mirror
```

```python
import functools

import jax
import jax.numpy as jnp
import numpy as np
from jax import lax
from jax.experimental import pallas as pl
from jax.experimental.pallas import tpu as pltpu
from jax.sharding import Mesh
from jax.sharding import PartitionSpec as P

MESH = pl.DeviceIdType.MESH
BF = jnp.bfloat16
F32 = jnp.float32
NB = 20
BP = 24
KB = 2 * BP
CG = 4
CW = NB // CG
PAIR_DEV = 2
MOST = 6
HALF = MOST // 2


def up(n, to):
    return -(-n // to) * to


def kernel(
    ny, nx, nz,
    tab, val, con, w_any, spread_d, mask_d, spread_m, mask_m, collect,
    out_d, out_m,
    w, call, vall, g, acc, prod, valp, pf, pp, rr, rp, rm, sp, sm, yb, xs, xr, ms, mr,
    bar_w, s_c, r_c, s_v, r_v,
    gs_p, gr_p, gs_m, gr_m, ss_s, ss_r,
    p_s, p_r, qs_p, qr_p, qs_m, qr_m,
    ys_p, yr_p, ys_m, yr_m, xs_s, xs_r, ms_s, ms_r,
):
    y, x, z, c = (lax.axis_index(a) for a in ("y", "x", "z", "c"))
    npb = ny * nx
    rows = 2 * nz
    me = y * nx + x
    row = z * 2 + c
    share = NB * NB // rows
    units = NB * CG // rows

    def at_pb(e):
        return (e // nx, lax.rem(e, nx), z, c)

    def at_row(r):
        return (y, x, r // 2, lax.rem(r, 2))

    def zrel(k):
        return lax.rem(z + k + 2 * nz, nz)

    def yrel(k):
        return lax.rem(y + k + 2 * ny, ny)

    barrier = pltpu.get_barrier_semaphore()

    @pl.loop(1, npb)
    def _(i):
        pl.semaphore_signal(barrier, inc=1, device_id=at_pb(lax.rem(me + i, npb)), device_id_type=MESH)

    @pl.loop(1, rows)
    def _(i):
        pl.semaphore_signal(barrier, inc=1, device_id=at_row(lax.rem(row + i, rows)), device_id_type=MESH)

    get_w = pltpu.make_async_copy(w_any.at[0], w, bar_w)
    get_w.start()

    def stage(buf, src):
        blank = jnp.zeros((BP - NB, 128), BF)
        for h in range(2):
            part = src[0, :, h * 128:(h + 1) * 128]
            buf[me, h * BP:(h + 1) * BP, :] = jnp.concatenate([part, blank], axis=0)

    stage(call, con)
    stage(vall, val)
    pl.semaphore_wait(barrier, npb - 1 + rows - 1)

    for buf, s_sem, r_sem in ((call, s_c, r_c), (vall, s_v, r_v)):
        @pl.loop(1, npb)
        def _(i, buf=buf, s_sem=s_sem, r_sem=r_sem):
            pltpu.make_async_remote_copy(
                src_ref=buf.at[me], dst_ref=buf.at[me], send_sem=s_sem, recv_sem=r_sem,
                device_id=at_pb(lax.rem(me + i, npb)), device_id_type=MESH,
            ).start()

    def all_of(buf, sem):
        ref = buf.at[pl.ds(0, npb - 1)]
        pltpu.make_async_copy(ref, ref, sem).wait()

    pf[:, units * NB:, :] = jnp.zeros((rows, pf.shape[1] - units * NB, 128), F32)

    @pl.loop(0, MOST)
    def _(s):
        acc[s] = jnp.zeros(acc.shape[1:], F32)

    all_of(call, r_c)

    @pl.loop(0, 2 * MOST)
    def _(i):
        g[row, i] = call[tab[me * 2 * MOST + i]]

    def gsend(d, t):
        r = zrel(-d * (t - 1)) * 2 + c
        blk = g.at[r]
        if t == nz // 2:
            blk = g.at[r, pl.ds(0 if d > 0 else MOST, MOST)]
        s_sem, r_sem = (gs_p, gr_p) if d > 0 else (gs_m, gr_m)
        return pltpu.make_async_remote_copy(
            src_ref=blk, dst_ref=blk, send_sem=s_sem.at[t - 1], recv_sem=r_sem.at[t - 1],
            device_id=(y, x, zrel(d), c), device_id_type=MESH,
        )

    def grecv(d, t):
        r = zrel(-d * t) * 2 + c
        blk = g.at[r]
        if t == nz // 2:
            blk = g.at[r, pl.ds(0 if d > 0 else MOST, MOST)]
        pltpu.make_async_copy(blk, blk, (gr_p if d > 0 else gr_m).at[t - 1]).wait()

    def sibling(zz, core):
        blk = g.at[zz * 2 + core]
        return pltpu.make_async_remote_copy(
            src_ref=blk, dst_ref=blk, send_sem=ss_s.at[zz], recv_sem=ss_r.at[zz],
            device_id=(y, x, z, 1 - c), device_id_type=MESH,
        )

    def block(zz):
        @pl.loop(0, MOST)
        def _(s):
            for core in range(2):
                for h in range(2):
                    lane = (core * 2 + h) * 128
                    one = g[zz * 2 + core, s, h * BP:(h + 1) * BP, :]
                    two = g[zz * 2 + core, MOST + s, h * BP:(h + 1) * BP, :]
                    for k in range(NB):
                        prod[k * BP:(k + 1) * BP, lane:lane + 128] = one[k:k + 1, :] * two
            cols = pl.ds(pl.multiple_of(zz * 512, 512), 512)
            acc[s] += lax.dot_general(
                prod[...], w[:, cols], (((1,), (1,)), ((), ())), preferred_element_type=F32
            )

    top = nz // 2
    gsend(1, 1).start()
    gsend(-1, 1).start()
    sibling(z, c).start()
    get_w.wait()
    for t in range(1, top + 1):
        if t == 1:
            sibling(z, 1 - c).wait_recv()
            block(z)
        elif t == top and top > 1:
            pass
        grecv(1, t)
        grecv(-1, t)
        if t < top:
            gsend(1, t + 1).start()
            gsend(-1, t + 1).start()
            sibling(zrel(-t), c).start()
            sibling(zrel(t), c).start()
        else:
            sibling(zrel(t), c).start()
        for k in ((-t, t) if t < top else (t,)):
            sibling(zrel(k), 1 - c).wait_recv()
            block(zrel(k))

    all_of(vall, r_v)

    @pl.loop(0, MOST)
    def _(s):
        one = vall[tab[me * 2 * MOST + s]]
        two = vall[tab[me * 2 * MOST + MOST + s]]
        for h in range(2):
            a, b = one[h * BP:(h + 1) * BP, :], two[h * BP:(h + 1) * BP, :]
            for k in range(NB):
                valp[k * BP:(k + 1) * BP, h * 128:(h + 1) * 128] = a[k:k + 1, :] * b
        for q in range(CG):
            it = jnp.concatenate(
                [acc[s, (q * CW + k) * BP:(q * CW + k) * BP + NB, :] for k in range(CW)]
                + [jnp.zeros((128 - CW * NB, 256), F32)], axis=0,
            ).astype(BF)
            part = lax.dot_general(valp[...], it, (((1,), (1,)), ((), ())), preferred_element_type=F32)
            for v in range(NB):
                u = v * CG + q
                r, i = u // units, u % units
                pf[r, i * NB:(i + 1) * NB, :] = part[v * BP:v * BP + NB, :]
        for r in range(rows):
            pp[s, r % 2, r // 2] = pf[r].astype(BF)
        pltpu.make_async_remote_copy(
            src_ref=pp.at[s, 1 - c], dst_ref=rr.at[s], send_sem=p_s.at[s], recv_sem=p_r.at[s],
            device_id=(y, x, z, 1 - c), device_id_type=MESH,
        ).start()

    def pair_copy(s):
        return pltpu.make_async_remote_copy(
            src_ref=pp.at[s, 1 - c], dst_ref=rr.at[s], send_sem=p_s.at[s], recv_sem=p_r.at[s],
            device_id=(y, x, z, 1 - c), device_id_type=MESH,
        )

    def qsend(d, t, s):
        out, into, s_sem, r_sem = (sp, rp, qs_p, qr_p) if d > 0 else (sm, rm, qs_m, qr_m)
        return pltpu.make_async_remote_copy(
            src_ref=out.at[t - 1, s], dst_ref=into.at[t - 1, s],
            send_sem=s_sem.at[t - 1, s], recv_sem=r_sem.at[t - 1, s],
            device_id=(y, x, zrel(d), c), device_id_type=MESH,
        )

    def first_half(d):
        return (0, HALF) if d > 0 else (HALF, MOST)

    def qstep(d, t, s, add):
        out, into = (sp, rp) if d > 0 else (sm, rm)
        own = pp[s, c, zrel(d * (top + 1 - t))]
        if add:
            qsend(d, t - 1, s).wait_recv()
            own = (own.astype(F32) + into[t - 2, s].astype(F32)).astype(BF)
        out[t - 1, s] = own
        qsend(d, t, s).start()

    def has(d, t, s):
        return t > 1 or first_half(d)[0] <= s < first_half(d)[1]

    for s in range(MOST):
        pair_copy(s).wait_recv()
        for zz in range(nz):
            pp[s, c, zz] = (pp[s, c, zz].astype(F32) + rr[s, zz].astype(F32)).astype(BF)
        for d in (1, -1):
            if has(d, 1, s):
                qstep(d, 1, s, False)
    for t in range(2, top + 1):
        for s in range(MOST):
            for d in (1, -1):
                qstep(d, t, s, has(d, t - 1, s))

    ytop = ny // 2

    def ysend(d, t, s):
        blk = yb.at[yrel(-d * (t - 1)), s]
        s_sem, r_sem = (ys_p, yr_p) if d > 0 else (ys_m, yr_m)
        return pltpu.make_async_remote_copy(
            src_ref=blk, dst_ref=blk, send_sem=s_sem.at[t - 1, s], recv_sem=r_sem.at[t - 1, s],
            device_id=(yrel(d), x, z, c), device_id_type=MESH,
        )

    def yhas(d, t, s):
        return t < ytop or first_half(d)[0] <= s < first_half(d)[1]

    def yrecv(d, t, s):
        blk = yb.at[yrel(-d * t), s]
        pltpu.make_async_copy(blk, blk, (yr_p if d > 0 else yr_m).at[t - 1, s]).wait()

    for s in range(MOST):
        total = pp[s, c, z].astype(F32)
        for d, into in ((1, rp), (-1, rm)):
            if has(d, top, s):
                qsend(d, top, s).wait_recv()
                total = total + into[top - 1, s].astype(F32)
        yb[y, s] = total.astype(BF)
        for d in (1, -1):
            if yhas(d, 1, s):
                ysend(d, 1, s).start()
    for t in range(1, ytop + 1):
        for s in range(MOST):
            for d in (1, -1):
                if yhas(d, t, s):
                    yrecv(d, t, s)
                    if t < ytop and yhas(d, t + 1, s):
                        ysend(d, t + 1, s).start()

    base = 2 * MOST * npb

    def xcopy(i):
        to = lax.rem(x + i, nx)
        return pltpu.make_async_remote_copy(
            src_ref=xs.at[to], dst_ref=xr.at[x], send_sem=xs_s.at[i], recv_sem=xs_r.at[i],
            device_id=(y, to, z, c), device_id_type=MESH,
        )

    for i in range(nx):
        to = lax.rem(x + i, nx)
        dest = xr if i == 0 else xs
        for j in range(2 * PAIR_DEV):
            pick = tab[base + (y * nx + to) * 4 + j]
            slot = tab[base + 4 * npb + (y * nx + to) * 4 + j]
            dest[to, j] = yb[pick, slot]
        if i:
            xcopy(i).start()
    for i in range(1, nx):
        xcopy(i).wait_recv()

    srows = xs.shape[2]
    at_r = lax.broadcasted_iota(jnp.int32, (srows, 128), 0)
    at_l = lax.broadcasted_iota(jnp.int32, (srows, 128), 1)

    def ordered(j, spread, mask):
        got = xr[tab[base + 8 * npb + me * 4 + j], j].astype(F32)
        kept = [
            jnp.where((at_r < units * NB) & (at_l >= k * NB) & (at_l < (k + 1) * NB), got, 0.0).astype(BF)
            for k in range(CW)
        ]
        parts = []
        for k in range(CW):
            wide = jnp.dot(kept[k], spread[...], preferred_element_type=F32)
            parts.append((wide * mask[...].astype(F32)).astype(BF))
        return jnp.dot(collect[...], jnp.concatenate(parts, axis=0), preferred_element_type=F32)

    rpad = up(share, 32)
    turned = jnp.concatenate(
        [ordered(PAIR_DEV + j, spread_m, mask_m) for j in range(PAIR_DEV)]
        + [jnp.zeros((128 - PAIR_DEV * rpad, rows * rpad), F32)], axis=0,
    ).T.astype(BF)
    for r in range(rows):
        ms[r] = turned[r * rpad:(r + 1) * rpad, :]
    mr[row] = ms[row]

    def mcopy(i):
        to = lax.rem(row + i, rows)
        return pltpu.make_async_remote_copy(
            src_ref=ms.at[to], dst_ref=mr.at[row], send_sem=ms_s.at[i], recv_sem=ms_r.at[i],
            device_id=at_row(to), device_id_type=MESH,
        )

    @pl.loop(1, rows)
    def _(i):
        mcopy(i).start()

    for j in range(PAIR_DEV):
        out_d[j] = ordered(j, spread_d, mask_d)[:share, :NB * NB].astype(BF)

    @pl.loop(1, rows)
    def _(i):
        mcopy(i).wait_recv()

    for j in range(PAIR_DEV):
        out_m[j] = jnp.concatenate(
            [mr[r].astype(F32)[:share, j * rpad:j * rpad + share] for r in range(rows)], axis=1
        ).astype(BF)

    all_of(call, s_c)
    all_of(vall, s_v)
    for t in range(1, top + 1):
        gsend(1, t).wait_send()
        gsend(-1, t).wait_send()
    for k in range(nz):
        sibling(k, c).wait_send()
    for s in range(MOST):
        pair_copy(s).wait_send()
        for t in range(1, top + 1):
            for d in (1, -1):
                if has(d, t, s):
                    qsend(d, t, s).wait_send()
        for t in range(1, ytop + 1):
            for d in (1, -1):
                if yhas(d, t, s):
                    ysend(d, t, s).wait_send()
    for i in range(1, nx):
        xcopy(i).wait_send()

    @pl.loop(1, rows)
    def _(i):
        mcopy(i).wait_send()


def constants(rows):
    share = NB * NB // rows
    units = NB * CG // rows
    srows = up(units * NB, 16)
    rpad = up(share, 32)
    lane = np.arange(128)
    plain = np.arange(up(NB * NB, 128))
    wd = np.where(plain < NB * NB, plain, -1)
    padded = np.arange(rows * rpad)
    wdm = np.where(padded % rpad < share, padded // rpad * share + padded % rpad, -1)
    r = np.arange(srows)

    def two(cols):
        spread = (lane[:, None] < CW * NB) & (cols[None, :] >= 0) & (lane[:, None] % NB == cols[None, :] % NB)
        mask = (r[:, None] < units * NB) & (cols[None, :] >= 0) & (r[:, None] % NB == cols[None, :] // NB)
        return spread, mask

    k = np.arange(CW * srows)
    out = np.arange(rpad)
    rr = k % srows
    collect = (
        (rr[None, :] < units * NB) & (out[:, None] < share)
        & (rr[None, :] // NB == out[:, None] // CW) & (k[None, :] // srows == out[:, None] % CW)
    )
    return [a.astype(np.float32).astype(BF) for a in (*two(wd), *two(wdm), collect)]


def table(pair_list, transfer_index, owner_map, npb):
    i32 = jnp.int32
    n = pair_list.shape[0]
    t = transfer_index[:, 0]
    p = jnp.arange(n, dtype=i32)
    ks = jnp.arange(owner_map.shape[0], dtype=i32)

    def owner(k):
        return jnp.sum(jnp.where(k[:, None] == ks[None, :], owner_map[None, :], 0), axis=1)

    def rank(labels):
        same = (labels[:, None] == labels[None, :]) & (p[None, :] < p[:, None])
        return jnp.sum(same.astype(i32), axis=1)

    first, second = owner(pair_list[:, 0]), owner(pair_list[:, 1])
    place = rank(t)
    q = jnp.arange(npb, dtype=i32)
    hit = (t[None, None, :] == q[:, None, None]) & (
        place[None, None, :] == jnp.arange(MOST, dtype=i32)[None, :, None]
    )
    one = jnp.sum(jnp.where(hit, first[None, None, :], 0), axis=2)
    two = jnp.sum(jnp.where(hit, second[None, None, :], 0), axis=2)
    j = jnp.arange(PAIR_DEV, dtype=i32)
    code = t * MOST + place
    hit_m = (second[None, None, :] == q[:, None, None]) & (rank(second)[None, None, :] == j[None, :, None])
    mirrored = jnp.sum(jnp.where(hit_m, code[None, None, :], 0), axis=2)
    want = jnp.concatenate([code.reshape(npb, PAIR_DEV), mirrored], axis=1)
    return one, two, want


def solution(mesh):
    sizes = tuple(int(np.prod([mesh.shape[a]])) for a in ("pb", "row"))
    nx, ny, nz = GRID.get(sizes, (4, 8, 8))
    split = Mesh(mesh.devices.reshape(ny, nx, nz, 2), ("y", "x", "z", "c"))
    npb, rows = ny * nx, 2 * nz
    share, units = NB * NB // rows, NB * CG // rows
    srows, rpad = up(units * NB, 16), up(share, 32)
    top, ytop = nz // 2, ny // 2
    dma = pltpu.SemaphoreType.DMA

    def shards(val, con, screened, pair_list, transfer_index, owner_map):
        one, two, want = table(pair_list, transfer_index, owner_map, npb)
        tab = jnp.concatenate([
            jnp.concatenate([one, two], axis=1).reshape(-1),
            (want // MOST // nx).reshape(-1), (want % MOST).reshape(-1), (want // MOST % nx).reshape(-1),
        ])
        consts = [jnp.asarray(a) for a in constants(rows)]
        vmem = pl.BlockSpec(memory_space=pltpu.VMEM)
        points = screened.shape[2]
        blk = (srows, 128)
        scratch = [
            pltpu.VMEM((256, points), BF),
            pltpu.VMEM((npb, KB, 128), BF),
            pltpu.VMEM((npb, KB, 128), BF),
            pltpu.VMEM((rows, 2 * MOST, KB, 128), BF),
            pltpu.VMEM((MOST, NB * BP, 256), F32),
            pltpu.VMEM((NB * BP, 512), BF),
            pltpu.VMEM((NB * BP, 256), BF),
            pltpu.VMEM((rows, *blk), F32),
            pltpu.VMEM((MOST, 2, nz, *blk), BF),
            pltpu.VMEM((MOST, nz, *blk), BF),
            *[pltpu.VMEM((top, MOST, *blk), BF) for _ in range(4)],
            pltpu.VMEM((ny, MOST, *blk), BF),
            pltpu.VMEM((nx, 4, *blk), BF),
            pltpu.VMEM((nx, 4, *blk), BF),
            pltpu.VMEM((rows, rpad, 128), BF),
            pltpu.VMEM((rows, rpad, 128), BF),
            dma, dma, dma, dma, dma,
            *[dma((top,)) for _ in range(4)],
            dma((nz,)), dma((nz,)),
            dma((MOST,)), dma((MOST,)),
            *[dma((top, MOST)) for _ in range(4)],
            *[dma((ytop, MOST)) for _ in range(4)],
            dma((nx,)), dma((nx,)), dma((rows,)), dma((rows,)),
        ]
        result = jax.ShapeDtypeStruct((PAIR_DEV, share, NB * NB), BF)
        return pl.pallas_call(
            functools.partial(kernel, ny, nx, nz),
            out_shape=(result, result),
            in_specs=[pl.BlockSpec(memory_space=pltpu.SMEM), vmem, vmem,
                      pl.BlockSpec(memory_space=pl.ANY), *[vmem] * 5],
            out_specs=(vmem, vmem),
            scratch_shapes=scratch,
            compiler_params=pltpu.CompilerParams(
                collective_id=0, has_side_effects=True, vmem_limit_bytes=50 * 2**20
            ),
        )(tab, val, con, screened, *consts)

    in_specs = (P(("y", "x"), None, ("z", "c")), P(("y", "x"), None, ("z", "c")),
                P(("y", "x"), ("z", "c"), None), P(), P(), P())
    out = P(("y", "x"), ("z", "c"), None)
    return jax.shard_map(shards, mesh=split, in_specs=in_specs, out_specs=(out, out), check_vma=False)


GRID = {(4, 4): (2, 2, 2), (2, 8): (1, 2, 4)}
```

```python
import functools

import jax
import jax.numpy as jnp
import numpy as np
from jax import lax
from jax.experimental import pallas as pl
from jax.experimental.pallas import tpu as pltpu
from jax.sharding import Mesh
from jax.sharding import PartitionSpec as P

MESH = pl.DeviceIdType.MESH
BF = jnp.bfloat16
F32 = jnp.float32
NB = 20
BP = 24
KB = 2 * BP
CG = 4
CW = NB // CG
PAIR_DEV = 2
MOST = 6
HALF = MOST // 2


def up(n, to):
    return -(-n // to) * to


def kernel(
    ny, nx, nz, pairs,
    tab, val_any, con_any, w_any, spread_d_any, mask_d_any, spread_m_any, mask_m_any, collect_any,
    out_d, out_m,
    val, con, w, spread_d, mask_d, spread_m, mask_m, collect,
    call, vall, g, acc, prod, valp, pf, pp, rr, rp, rm, sp, sm, yb, xs, xr_d, xr_m, ms, mr,
    loc_t, loc,
    bx_s, bx_r, bs_p, br_p, bs_m, br_m,
    gs_p, gr_p, gs_m, gr_m, ss_s, ss_r,
    p_s, p_r, qs_p, qr_p, qs_m, qr_m,
    ys_p, yr_p, ys_m, yr_m, xs_s, xs_r, ms_s, ms_r,
):
    y, x, z, c = (lax.axis_index(a) for a in ("y", "x", "z", "c"))
    rows = 2 * nz
    me = y * nx + x
    row = z * 2 + c
    share = NB * NB // rows
    units = NB * CG // rows
    top, ytop = nz // 2, ny // 2

    def at_row(r):
        return (y, x, r // 2, lax.rem(r, 2))

    def zrel(k):
        return lax.rem(z + k + 2 * nz, nz)

    def yrel(k):
        return lax.rem(y + k + 2 * ny, ny)

    def xrel(k):
        return lax.rem(x + k + 2 * nx, nx)

    barrier = pltpu.get_barrier_semaphore()
    for i in range(1, nx):
        pl.semaphore_signal(barrier, inc=1, device_id=(y, xrel(i), z, c), device_id_type=MESH)
    for d in (1, -1):
        pl.semaphore_signal(barrier, inc=1, device_id=(yrel(d), x, z, c), device_id_type=MESH)

    @pl.loop(1, rows)
    def _(i):
        pl.semaphore_signal(barrier, inc=1, device_id=at_row(lax.rem(row + i, rows)), device_id_type=MESH)

    fetch = [
        pltpu.make_async_copy(a, b, loc.at[i])
        for i, (a, b) in enumerate((
            (con_any, con), (val_any, val), (w_any.at[0], w), (spread_d_any, spread_d), (mask_d_any, mask_d),
            (spread_m_any, spread_m), (mask_m_any, mask_m), (collect_any, collect),
        ))
    ]
    for f in fetch:
        f.start()

    def stage(buf, src):
        blank = jnp.zeros((BP - NB, 128), BF)
        for h in range(2):
            part = src[0, :, h * 128:(h + 1) * 128]
            buf[y, x, h * BP:(h + 1) * BP, :] = jnp.concatenate([part, blank], axis=0)

    fetch[0].wait()
    stage(call, con)
    fetch[1].wait()
    stage(vall, val)
    pl.semaphore_wait(barrier, nx - 1 + 2 + rows - 1)

    def bx(n, i):
        ref = (call, vall)[n].at[y, x]
        return pltpu.make_async_remote_copy(
            src_ref=ref, dst_ref=ref, send_sem=bx_s.at[n, i], recv_sem=bx_r.at[n, i],
            device_id=(y, xrel(i), z, c), device_id_type=MESH,
        )

    def bx_recv(n, i):
        ref = (call, vall)[n].at[y, xrel(-i)]
        pltpu.make_async_copy(ref, ref, bx_r.at[n, i]).wait()

    def b_has(d, t, i):
        return t < ytop or (i < nx // 2 if d > 0 else i >= nx // 2)

    def by(n, d, t, i):
        ref = (call, vall)[n].at[yrel(-d * (t - 1)), xrel(-i)]
        s_sem, r_sem = (bs_p, br_p) if d > 0 else (bs_m, br_m)
        return pltpu.make_async_remote_copy(
            src_ref=ref, dst_ref=ref, send_sem=s_sem.at[n, t - 1, i], recv_sem=r_sem.at[n, t - 1, i],
            device_id=(yrel(d), x, z, c), device_id_type=MESH,
        )

    def by_recv(n, d, t, i):
        ref = (call, vall)[n].at[yrel(-d * t), xrel(-i)]
        pltpu.make_async_copy(ref, ref, (br_p if d > 0 else br_m).at[n, t - 1, i]).wait()

    def by_first(n):
        for i in range(nx):
            if i:
                bx_recv(n, i)
            for d in (1, -1):
                if b_has(d, 1, i):
                    by(n, d, 1, i).start()

    def by_step(n, t):
        for i in range(nx):
            for d in (1, -1):
                if b_has(d, t, i):
                    by_recv(n, d, t, i)
                    if t < ytop and b_has(d, t + 1, i):
                        by(n, d, t + 1, i).start()

    for n in range(2):
        for i in range(1, nx):
            bx(n, i).start()
    by_first(0)

    pf[:, units * NB:, :] = jnp.zeros((rows, pf.shape[1] - units * NB, 128), F32)

    @pl.loop(0, MOST)
    def _(s):
        acc[s] = jnp.zeros(acc.shape[1:], F32)

    def owner(k):
        return tab[3 * pairs + k]

    def own_slots(p, carry):
        count, slots = carry
        hit = tab[p] == me
        slots = tuple(jnp.where(hit & (count == s), p, slots[s]) for s in range(MOST))
        return count + hit.astype(jnp.int32), slots

    zero = jnp.int32(0)
    _, slots = lax.fori_loop(0, pairs, own_slots, (zero, (zero,) * MOST))
    first = [owner(tab[pairs + p]) for p in slots]
    second = [owner(tab[2 * pairs + p]) for p in slots]

    def by_second(p, carry):
        e = owner(tab[2 * pairs + p])
        new = []
        for k in range(nx):
            count, one, two = carry[k]
            hit = e == y * nx + k
            new.append((count + hit.astype(jnp.int32), jnp.where(hit & (count == 0), p, one),
                        jnp.where(hit & (count == 1), p, two)))
        return tuple(new)

    found = lax.fori_loop(0, pairs, by_second, ((zero,) * 3,) * nx)
    wanted = []
    for k in range(nx):
        at = (y * nx + k) * PAIR_DEV
        wanted += [at, at + 1, found[k][1], found[k][2]]
    column = [tab[p] for p in wanted]

    def ranks(p, carry):
        return tuple(
            n + ((tab[p] == q) & (p < own)).astype(jnp.int32) for n, q, own in zip(carry, column, wanted)
        )

    ranked = lax.fori_loop(0, pairs, ranks, (zero,) * len(wanted))
    for i in range(4 * nx):
        loc_t[i] = lax.div(column[i], nx)
        loc_t[4 * nx + i] = jnp.minimum(ranked[i], MOST - 1)
        loc_t[8 * nx + i] = lax.rem(column[i], nx)

    for t in range(1, ytop + 1):
        by_step(0, t)

    for i, k in enumerate(first + second):
        g[row, i] = call[lax.div(k, nx), lax.rem(k, nx)]

    def g_has(d, t, h):
        return t < top or h == (0 if d > 0 else 1)

    def g_ref(k, h):
        return g.at[zrel(k) * 2 + c, pl.ds(h * MOST, MOST)]

    def gsend(d, t, h):
        ref = g_ref(-d * (t - 1), h)
        s_sem, r_sem = (gs_p, gr_p) if d > 0 else (gs_m, gr_m)
        return pltpu.make_async_remote_copy(
            src_ref=ref, dst_ref=ref, send_sem=s_sem.at[t - 1, h], recv_sem=r_sem.at[t - 1, h],
            device_id=(y, x, zrel(d), c), device_id_type=MESH,
        )

    def grecv(d, t, h):
        ref = g_ref(-d * t, h)
        pltpu.make_async_copy(ref, ref, (gr_p if d > 0 else gr_m).at[t - 1, h]).wait()

    def sibling(zz, core, h):
        ref = g.at[zz * 2 + core, pl.ds(h * MOST, MOST)]
        return pltpu.make_async_remote_copy(
            src_ref=ref, dst_ref=ref, send_sem=ss_s.at[zz, h], recv_sem=ss_r.at[zz, h],
            device_id=(y, x, z, 1 - c), device_id_type=MESH,
        )

    def block(zz):
        for h in range(2):
            sibling(zz, 1 - c, h).wait_recv()

        @pl.loop(0, MOST)
        def _(s):
            for core in range(2):
                for h in range(2):
                    lane = (core * 2 + h) * 128
                    one = g[zz * 2 + core, s, h * BP:(h + 1) * BP, :]
                    two = g[zz * 2 + core, MOST + s, h * BP:(h + 1) * BP, :]
                    for k in range(NB):
                        prod[k * BP:(k + 1) * BP, lane:lane + 128] = one[k:k + 1, :] * two
            cols = pl.ds(pl.multiple_of(zz * 512, 512), 512)
            acc[s] += lax.dot_general(
                prod[...], w[:, cols], (((1,), (1,)), ((), ())), preferred_element_type=F32
            )

    for h in range(2):
        for d in (1, -1):
            if g_has(d, 1, h):
                gsend(d, 1, h).start()
        sibling(z, c, h).start()
    by_first(1)
    fetch[2].wait()
    before = [z]
    for t in range(1, top + 1):
        for h in range(2):
            for d in (1, -1):
                if g_has(d, t, h):
                    grecv(d, t, h)
                    if t < top and g_has(d, t + 1, h):
                        gsend(d, t + 1, h).start()
                    sibling(zrel(-d * t), c, h).start()
            if h < len(before):
                block(before[h])
        before = [zrel(-t), zrel(t)] if t < top else [zrel(t)]
        if t <= ytop:
            by_step(1, t)
    for t in range(top + 1, ytop + 1):
        by_step(1, t)
    for zz in before:
        block(zz)

    def pair_copy(s):
        return pltpu.make_async_remote_copy(
            src_ref=pp.at[s, 1 - c], dst_ref=rr.at[s], send_sem=p_s.at[s], recv_sem=p_r.at[s],
            device_id=(y, x, z, 1 - c), device_id_type=MESH,
        )

    def partial(s):
        one = vall[lax.div(first[s], nx), lax.rem(first[s], nx)]
        two = vall[lax.div(second[s], nx), lax.rem(second[s], nx)]
        for h in range(2):
            a, b = one[h * BP:(h + 1) * BP, :], two[h * BP:(h + 1) * BP, :]
            for k in range(NB):
                valp[k * BP:(k + 1) * BP, h * 128:(h + 1) * 128] = a[k:k + 1, :] * b
        for q in range(CG):
            it = jnp.concatenate(
                [acc[s, (q * CW + k) * BP:(q * CW + k) * BP + NB, :] for k in range(CW)]
                + [jnp.zeros((128 - CW * NB, 256), F32)], axis=0,
            ).astype(BF)
            part = lax.dot_general(valp[...], it, (((1,), (1,)), ((), ())), preferred_element_type=F32)
            for v in range(NB):
                u = v * CG + q
                r, i = u // units, u % units
                pf[r, i * NB:(i + 1) * NB, :] = part[v * BP:v * BP + NB, :]
        for r in range(rows):
            pp[s, r % 2, r // 2] = pf[r].astype(BF)
        pair_copy(s).start()

    def qsend(d, t, s):
        out, into, s_sem, r_sem = (sp, rp, qs_p, qr_p) if d > 0 else (sm, rm, qs_m, qr_m)
        return pltpu.make_async_remote_copy(
            src_ref=out.at[t - 1, s], dst_ref=into.at[t - 1, s],
            send_sem=s_sem.at[t - 1, s], recv_sem=r_sem.at[t - 1, s],
            device_id=(y, x, zrel(d), c), device_id_type=MESH,
        )

    def first_half(d):
        return (0, HALF) if d > 0 else (HALF, MOST)

    def has(d, t, s):
        return t > 1 or first_half(d)[0] <= s < first_half(d)[1]

    def qstep(d, t, s, add):
        out, into = (sp, rp) if d > 0 else (sm, rm)
        own = pp[s, c, zrel(d * (top + 1 - t))]
        if add:
            qsend(d, t - 1, s).wait_recv()
            own = (own.astype(F32) + into[t - 2, s].astype(F32)).astype(BF)
        out[t - 1, s] = own
        qsend(d, t, s).start()

    def added(s):
        pair_copy(s).wait_recv()

        @pl.loop(0, nz)
        def _(zz):
            pp[s, c, zz] = (pp[s, c, zz].astype(F32) + rr[s, zz].astype(F32)).astype(BF)

        for d in (1, -1):
            if has(d, 1, s):
                qstep(d, 1, s, False)
            elif top > 1:
                qstep(d, 2, s, False)

    def ysend(d, t, s):
        blk = yb.at[yrel(-d * (t - 1)), s]
        s_sem, r_sem = (ys_p, yr_p) if d > 0 else (ys_m, yr_m)
        return pltpu.make_async_remote_copy(
            src_ref=blk, dst_ref=blk, send_sem=s_sem.at[t - 1, s], recv_sem=r_sem.at[t - 1, s],
            device_id=(yrel(d), x, z, c), device_id_type=MESH,
        )

    def yhas(d, t, s):
        return t < ytop or first_half(d)[0] <= s < first_half(d)[1]

    def yrecv(d, t, s):
        blk = yb.at[yrel(-d * t), s]
        pltpu.make_async_copy(blk, blk, (yr_p if d > 0 else yr_m).at[t - 1, s]).wait()

    def done(s):
        total = pp[s, c, z].astype(F32)
        for d, into in ((1, rp), (-1, rm)):
            if has(d, top, s):
                qsend(d, top, s).wait_recv()
                total = total + into[top - 1, s].astype(F32)
        yb[y, s] = total.astype(BF)
        for d in (1, -1):
            if yhas(d, 1, s):
                ysend(d, 1, s).start()

    def ystep(t, s):
        for d in (1, -1):
            if yhas(d, t, s):
                yrecv(d, t, s)
                if t < ytop and yhas(d, t + 1, s):
                    ysend(d, t + 1, s).start()

    stages = [partial, added]
    for t in range(2, top + 1):
        def stage_q(s, t=t):
            for d in (1, -1):
                if t > 2 or has(d, 1, s):
                    qstep(d, t, s, True)
        stages.append(stage_q)
    stages.append(done)
    for t in range(1, ytop + 1):
        stages.append(functools.partial(ystep, t))
    for step in range(MOST + len(stages) - 1):
        for k in reversed(range(len(stages))):
            if 0 <= step - k < MOST:
                stages[k](step - k)

    def xcopy(i, m):
        to = xrel(i)
        part = pl.ds(m * PAIR_DEV, PAIR_DEV)
        return pltpu.make_async_remote_copy(
            src_ref=xs.at[to, part], dst_ref=(xr_d, xr_m)[m].at[x], send_sem=xs_s.at[m, i], recv_sem=xs_r.at[m, i],
            device_id=(y, to, z, c), device_id_type=MESH,
        )

    for m in (1, 0):
        for i in list(range(1, nx)) + [0]:
            to = xrel(i)
            for j in range(m * PAIR_DEV, (m + 1) * PAIR_DEV):
                got = yb[loc_t[to * 4 + j], loc_t[4 * nx + to * 4 + j]]
                if i:
                    xs[to, j] = got
                else:
                    (xr_d, xr_m)[m][to, j - m * PAIR_DEV] = got
            if i:
                xcopy(i, m).start()

    for f in fetch[3:]:
        f.wait()
    for i in range(1, nx):
        xcopy(i, 1).wait_recv()

    srows = xs.shape[2]
    at_r = lax.broadcasted_iota(jnp.int32, (srows, 128), 0)
    at_l = lax.broadcasted_iota(jnp.int32, (srows, 128), 1)

    def ordered(m, j, spread, mask):
        got = (xr_d, xr_m)[m][loc_t[8 * nx + x * 4 + m * PAIR_DEV + j], j].astype(F32)
        kept = [
            jnp.where((at_r < units * NB) & (at_l >= k * NB) & (at_l < (k + 1) * NB), got, 0.0).astype(BF)
            for k in range(CW)
        ]
        parts = []
        for k in range(CW):
            wide = jnp.dot(kept[k], spread[...], preferred_element_type=F32)
            parts.append((wide * mask[...].astype(F32)).astype(BF))
        return jnp.dot(collect[...], jnp.concatenate(parts, axis=0), preferred_element_type=F32)

    rpad = up(share, 32)
    turned = jnp.concatenate(
        [ordered(1, j, spread_m, mask_m) for j in range(PAIR_DEV)]
        + [jnp.zeros((128 - PAIR_DEV * rpad, rows * rpad), F32)], axis=0,
    ).T.astype(BF)
    for r in range(rows):
        ms[r] = turned[r * rpad:(r + 1) * rpad, :]
    mr[row] = ms[row]

    def mcopy(i):
        to = lax.rem(row + i, rows)
        return pltpu.make_async_remote_copy(
            src_ref=ms.at[to], dst_ref=mr.at[row], send_sem=ms_s.at[i], recv_sem=ms_r.at[i],
            device_id=at_row(to), device_id_type=MESH,
        )

    @pl.loop(1, rows)
    def _(i):
        mcopy(i).start()

    for i in range(1, nx):
        xcopy(i, 0).wait_recv()
    for j in range(PAIR_DEV):
        out_d[j] = ordered(0, j, spread_d, mask_d)[:share, :NB * NB].astype(BF)

    @pl.loop(1, rows)
    def _(i):
        mcopy(i).wait_recv()

    for j in range(PAIR_DEV):
        out_m[j] = jnp.concatenate(
            [mr[r].astype(F32)[:share, j * rpad:j * rpad + share] for r in range(rows)], axis=1
        ).astype(BF)

    for n in range(2):
        for i in range(1, nx):
            bx(n, i).wait_send()
        for t in range(1, ytop + 1):
            for i in range(nx):
                for d in (1, -1):
                    if b_has(d, t, i):
                        by(n, d, t, i).wait_send()
    for h in range(2):
        for t in range(1, top + 1):
            for d in (1, -1):
                if g_has(d, t, h):
                    gsend(d, t, h).wait_send()
        for k in range(nz):
            sibling(k, c, h).wait_send()
    for s in range(MOST):
        pair_copy(s).wait_send()
        for t in range(1, top + 1):
            for d in (1, -1):
                if has(d, t, s):
                    qsend(d, t, s).wait_send()
        for t in range(1, ytop + 1):
            for d in (1, -1):
                if yhas(d, t, s):
                    ysend(d, t, s).wait_send()
    for m in range(2):
        for i in range(1, nx):
            xcopy(i, m).wait_send()

    @pl.loop(1, rows)
    def _(i):
        mcopy(i).wait_send()


def constants(rows):
    share = NB * NB // rows
    units = NB * CG // rows
    srows = up(units * NB, 16)
    rpad = up(share, 32)
    lane = np.arange(128)
    plain = np.arange(up(NB * NB, 128))
    wd = np.where(plain < NB * NB, plain, -1)
    padded = np.arange(rows * rpad)
    wdm = np.where(padded % rpad < share, padded // rpad * share + padded % rpad, -1)
    r = np.arange(srows)

    def two(cols):
        spread = (lane[:, None] < CW * NB) & (cols[None, :] >= 0) & (lane[:, None] % NB == cols[None, :] % NB)
        mask = (r[:, None] < units * NB) & (cols[None, :] >= 0) & (r[:, None] % NB == cols[None, :] // NB)
        return spread, mask

    k = np.arange(CW * srows)
    out = np.arange(rpad)
    rr = k % srows
    collect = (
        (rr[None, :] < units * NB) & (out[:, None] < share)
        & (rr[None, :] // NB == out[:, None] // CW) & (k[None, :] // srows == out[:, None] % CW)
    )
    return [a.astype(np.float32).astype(BF) for a in (*two(wd), *two(wdm), collect)]


def solution(mesh):
    sizes = tuple(int(np.prod([mesh.shape[a]])) for a in ("pb", "row"))
    nx, ny, nz = GRID.get(sizes, (4, 8, 8))
    split = Mesh(mesh.devices.reshape(ny, nx, nz, 2), ("y", "x", "z", "c"))
    npb, rows = ny * nx, 2 * nz
    share, units = NB * NB // rows, NB * CG // rows
    srows, rpad = up(units * NB, 16), up(share, 32)
    top, ytop = nz // 2, ny // 2
    dma = pltpu.SemaphoreType.DMA

    def shards(val, con, screened, pair_list, transfer_index, owner_map):
        pairs = pair_list.shape[0]
        tab = jnp.concatenate([transfer_index[:, 0], pair_list[:, 0], pair_list[:, 1], owner_map])
        consts = [jnp.asarray(a) for a in constants(rows)]
        vmem, anywhere = pl.BlockSpec(memory_space=pltpu.VMEM), pl.BlockSpec(memory_space=pl.ANY)
        points = screened.shape[2]
        blk = (srows, 128)
        scratch = [
            pltpu.VMEM(val.shape, BF), pltpu.VMEM(con.shape, BF),
            pltpu.VMEM((256, points), BF),
            *[pltpu.VMEM(a.shape, BF) for a in consts],
            pltpu.VMEM((ny, nx, KB, 128), BF),
            pltpu.VMEM((ny, nx, KB, 128), BF),
            pltpu.VMEM((rows, 2 * MOST, KB, 128), BF),
            pltpu.VMEM((MOST, NB * BP, 256), F32),
            pltpu.VMEM((NB * BP, 512), BF),
            pltpu.VMEM((NB * BP, 256), BF),
            pltpu.VMEM((rows, *blk), F32),
            pltpu.VMEM((MOST, 2, nz, *blk), BF),
            pltpu.VMEM((MOST, nz, *blk), BF),
            *[pltpu.VMEM((top, MOST, *blk), BF) for _ in range(4)],
            pltpu.VMEM((ny, MOST, *blk), BF),
            pltpu.VMEM((nx, 2 * PAIR_DEV, *blk), BF),
            pltpu.VMEM((nx, PAIR_DEV, *blk), BF),
            pltpu.VMEM((nx, PAIR_DEV, *blk), BF),
            pltpu.VMEM((rows, rpad, 128), BF),
            pltpu.VMEM((rows, rpad, 128), BF),
            pltpu.SMEM((12 * nx,), jnp.int32),
            dma((8,)),
            dma((2, nx)), dma((2, nx)),
            *[dma((2, ytop, nx)) for _ in range(4)],
            *[dma((top, 2)) for _ in range(4)],
            dma((nz, 2)), dma((nz, 2)),
            dma((MOST,)), dma((MOST,)),
            *[dma((top, MOST)) for _ in range(4)],
            *[dma((ytop, MOST)) for _ in range(4)],
            dma((2, nx)), dma((2, nx)), dma((rows,)), dma((rows,)),
        ]
        result = jax.ShapeDtypeStruct((PAIR_DEV, share, NB * NB), BF)
        return pl.pallas_call(
            functools.partial(kernel, ny, nx, nz, pairs),
            out_shape=(result, result),
            in_specs=[pl.BlockSpec(memory_space=pltpu.SMEM), *[anywhere] * 8],
            out_specs=(vmem, vmem),
            scratch_shapes=scratch,
            compiler_params=pltpu.CompilerParams(
                collective_id=0, has_side_effects=True, vmem_limit_bytes=60 * 2**20
            ),
        )(tab, val, con, screened, *consts)

    in_specs = (P(("y", "x"), None, ("z", "c")), P(("y", "x"), None, ("z", "c")),
                P(("y", "x"), ("z", "c"), None), P(), P(), P())
    out = P(("y", "x"), ("z", "c"), None)
    return jax.shard_map(shards, mesh=split, in_specs=in_specs, out_specs=(out, out), check_vma=False)


GRID = {(4, 4): (2, 2, 2), (2, 8): (1, 2, 4)}
```

```python
import functools

import jax
import jax.numpy as jnp
import numpy as np
from jax import lax
from jax.experimental import pallas as pl
from jax.experimental.pallas import tpu as pltpu
from jax.sharding import Mesh
from jax.sharding import PartitionSpec as P

MESH = pl.DeviceIdType.MESH
BF = jnp.bfloat16
F32 = jnp.float32
NB = 20
BP = 24
KB = 2 * BP
CG = 4
CW = NB // CG
PAIR_DEV = 2
MOST = 6
HALF = MOST // 2
CHUNKS = 4


def up(n, to):
    return -(-n // to) * to


def kernel(
    ny, nx, nz, pairs,
    tab, val_any, con_any, w_any, spread_d_any, mask_d_any, spread_m_any, mask_m_any, collect_any,
    out_d, out_m,
    val, con, w, spread_d, mask_d, spread_m, mask_m, collect,
    call, vall, g, acc, prod, valp, pf, pp, rr, rp, rm, sp, sm, yb, xs, xr_d, xr_m, ms, mr,
    loc_t, loc,
    by_s, by_r, bx_s, bx_r,
    gs_p, gr_p, gs_m, gr_m, ss_s, ss_r,
    p_s, p_r, qs_p, qr_p, qs_m, qr_m,
    ys_p, yr_p, ys_m, yr_m, xs_s, xs_r, ms_s, ms_r,
):
    y, x, z, c = (lax.axis_index(a) for a in ("y", "x", "z", "c"))
    rows = 2 * nz
    me = y * nx + x
    row = z * 2 + c
    share = NB * NB // rows
    units = NB * CG // rows
    top, ytop = nz // 2, ny // 2

    def at_row(r):
        return (y, x, r // 2, lax.rem(r, 2))

    def zrel(k):
        return lax.rem(z + k + 2 * nz, nz)

    def yrel(k):
        return lax.rem(y + k + 2 * ny, ny)

    def xrel(k):
        return lax.rem(x + k + 2 * nx, nx)

    barrier = pltpu.get_barrier_semaphore()
    for i in range(1, nx):
        pl.semaphore_signal(barrier, inc=1, device_id=(y, xrel(i), z, c), device_id_type=MESH)
    for i in range(1, ny):
        pl.semaphore_signal(barrier, inc=1, device_id=(yrel(i), x, z, c), device_id_type=MESH)

    @pl.loop(1, rows)
    def _(i):
        pl.semaphore_signal(barrier, inc=1, device_id=at_row(lax.rem(row + i, rows)), device_id_type=MESH)

    fetch = [
        pltpu.make_async_copy(a, b, loc.at[i])
        for i, (a, b) in enumerate((
            (con_any, con), (val_any, val), (w_any.at[0], w), (spread_d_any, spread_d), (mask_d_any, mask_d),
            (spread_m_any, spread_m), (mask_m_any, mask_m), (collect_any, collect),
        ))
    ]
    for f in fetch:
        f.start()

    def stage(buf, src):
        blank = jnp.zeros((BP - NB, 128), BF)
        for h in range(2):
            part = src[0, :, h * 128:(h + 1) * 128]
            buf[y, x, h * BP:(h + 1) * BP, :] = jnp.concatenate([part, blank], axis=0)

    fetch[0].wait()
    stage(call, con)
    fetch[1].wait()
    stage(vall, val)
    pl.semaphore_wait(barrier, nx - 1 + ny - 1 + rows - 1)

    near = sorted(range(1, ny), key=lambda i: min(i, ny - i))

    def by(n, i):
        ref = (call, vall)[n].at[y, x]
        return pltpu.make_async_remote_copy(
            src_ref=ref, dst_ref=ref, send_sem=by_s.at[n, i], recv_sem=by_r.at[n, i],
            device_id=(yrel(i), x, z, c), device_id_type=MESH,
        )

    def bx(n, i, k):
        ref = (call, vall)[n].at[yrel(-i), x]
        return pltpu.make_async_remote_copy(
            src_ref=ref, dst_ref=ref, send_sem=bx_s.at[n, i, k], recv_sem=bx_r.at[n, i, k],
            device_id=(y, xrel(k), z, c), device_id_type=MESH,
        )

    def b_arrived(n, i, k):
        ref = (call, vall)[n].at[yrel(-i), xrel(-k)]
        pltpu.make_async_copy(ref, ref, bx_r.at[n, i, k] if k else by_r.at[n, i]).wait()

    def pass_on(n, i):
        if i:
            b_arrived(n, i, 0)
        for k in range(1, nx):
            bx(n, i, k).start()

    def all_arrived(n):
        for i in [0] + near:
            for k in range(1, nx):
                b_arrived(n, i, k)

    pass_on(0, 0)
    for n in range(2):
        for i in near:
            by(n, i).start()

    pf[:, units * NB:, :] = jnp.zeros((rows, pf.shape[1] - units * NB, 128), F32)

    @pl.loop(0, MOST)
    def _(s):
        acc[s] = jnp.zeros(acc.shape[1:], F32)

    for i in near:
        pass_on(0, i)

    def owner(k):
        return tab[3 * pairs + k]

    def own_slots(p, carry):
        count, slots = carry
        hit = tab[p] == me
        slots = tuple(jnp.where(hit & (count == s), p, slots[s]) for s in range(MOST))
        return count + hit.astype(jnp.int32), slots

    zero = jnp.int32(0)
    _, slots = lax.fori_loop(0, pairs, own_slots, (zero, (zero,) * MOST))
    first = [owner(tab[pairs + p]) for p in slots]
    second = [owner(tab[2 * pairs + p]) for p in slots]

    def by_second(p, carry):
        e = owner(tab[2 * pairs + p])
        new = []
        for k in range(nx):
            count, one, two = carry[k]
            hit = e == y * nx + k
            new.append((count + hit.astype(jnp.int32), jnp.where(hit & (count == 0), p, one),
                        jnp.where(hit & (count == 1), p, two)))
        return tuple(new)

    found = lax.fori_loop(0, pairs, by_second, ((zero,) * 3,) * nx)
    wanted = []
    for k in range(nx):
        at = (y * nx + k) * PAIR_DEV
        wanted += [at, at + 1, found[k][1], found[k][2]]
    column = [tab[p] for p in wanted]

    def ranks(p, carry):
        return tuple(
            n + ((tab[p] == q) & (p < own)).astype(jnp.int32) for n, q, own in zip(carry, column, wanted)
        )

    ranked = lax.fori_loop(0, pairs, ranks, (zero,) * len(wanted))
    for i in range(4 * nx):
        loc_t[i] = lax.div(column[i], nx)
        loc_t[4 * nx + i] = jnp.minimum(ranked[i], MOST - 1)
        loc_t[8 * nx + i] = lax.rem(column[i], nx)

    for i in [0] + near:
        pass_on(1, i)
    all_arrived(0)

    for i, k in enumerate(first + second):
        g[row, i] = call[lax.div(k, nx), lax.rem(k, nx)]

    def g_has(d, t, h):
        return t < top or (h < CHUNKS // 2) == (d > 0)

    def g_ref(k, h):
        return g.at[zrel(k) * 2 + c, pl.ds(h * (2 * MOST // CHUNKS), 2 * MOST // CHUNKS)]

    def gsend(d, t, h):
        ref = g_ref(-d * (t - 1), h)
        s_sem, r_sem = (gs_p, gr_p) if d > 0 else (gs_m, gr_m)
        return pltpu.make_async_remote_copy(
            src_ref=ref, dst_ref=ref, send_sem=s_sem.at[t - 1, h], recv_sem=r_sem.at[t - 1, h],
            device_id=(y, x, zrel(d), c), device_id_type=MESH,
        )

    def grecv(d, t, h):
        ref = g_ref(-d * t, h)
        pltpu.make_async_copy(ref, ref, (gr_p if d > 0 else gr_m).at[t - 1, h]).wait()

    def sibling(zz, core, h):
        ref = g.at[zz * 2 + core, pl.ds(h * MOST, MOST)]
        return pltpu.make_async_remote_copy(
            src_ref=ref, dst_ref=ref, send_sem=ss_s.at[zz, h], recv_sem=ss_r.at[zz, h],
            device_id=(y, x, z, 1 - c), device_id_type=MESH,
        )

    def block(zz):
        for h in range(2):
            sibling(zz, 1 - c, h).wait_recv()

        @pl.loop(0, MOST)
        def _(s):
            for core in range(2):
                for h in range(2):
                    lane = (core * 2 + h) * 128
                    one = g[zz * 2 + core, s, h * BP:(h + 1) * BP, :]
                    two = g[zz * 2 + core, MOST + s, h * BP:(h + 1) * BP, :]
                    for k in range(NB):
                        prod[k * BP:(k + 1) * BP, lane:lane + 128] = one[k:k + 1, :] * two
            cols = pl.ds(pl.multiple_of(zz * 512, 512), 512)
            acc[s] += lax.dot_general(
                prod[...], w[:, cols], (((1,), (1,)), ((), ())), preferred_element_type=F32
            )

    for h in range(CHUNKS):
        for d in (1, -1):
            if g_has(d, 1, h):
                gsend(d, 1, h).start()
    for h in range(2):
        sibling(z, c, h).start()
    fetch[2].wait()
    before = [z]
    for t in range(1, top + 1):
        for h in range(CHUNKS):
            for d in (1, -1):
                if g_has(d, t, h):
                    grecv(d, t, h)
                    if t < top and g_has(d, t + 1, h):
                        gsend(d, t + 1, h).start()
            if (h + 1) % (CHUNKS // 2) == 0:
                half = (h + 1) // (CHUNKS // 2) - 1
                for d in (1, -1):
                    if g_has(d, t, h):
                        sibling(zrel(-d * t), c, half).start()
                if half < len(before):
                    block(before[half])
        before = [zrel(-t), zrel(t)] if t < top else [zrel(t)]
    for zz in before:
        block(zz)
    all_arrived(1)

    def pair_copy(s):
        return pltpu.make_async_remote_copy(
            src_ref=pp.at[s, 1 - c], dst_ref=rr.at[s], send_sem=p_s.at[s], recv_sem=p_r.at[s],
            device_id=(y, x, z, 1 - c), device_id_type=MESH,
        )

    def partial(s):
        one = vall[lax.div(first[s], nx), lax.rem(first[s], nx)]
        two = vall[lax.div(second[s], nx), lax.rem(second[s], nx)]
        for h in range(2):
            a, b = one[h * BP:(h + 1) * BP, :], two[h * BP:(h + 1) * BP, :]
            for k in range(NB):
                valp[k * BP:(k + 1) * BP, h * 128:(h + 1) * 128] = a[k:k + 1, :] * b
        for q in range(CG):
            it = jnp.concatenate(
                [acc[s, (q * CW + k) * BP:(q * CW + k) * BP + NB, :] for k in range(CW)]
                + [jnp.zeros((128 - CW * NB, 256), F32)], axis=0,
            ).astype(BF)
            part = lax.dot_general(valp[...], it, (((1,), (1,)), ((), ())), preferred_element_type=F32)
            for v in range(NB):
                u = v * CG + q
                r, i = u // units, u % units
                pf[r, i * NB:(i + 1) * NB, :] = part[v * BP:v * BP + NB, :]
        for r in range(rows):
            pp[s, r % 2, r // 2] = pf[r].astype(BF)
        pair_copy(s).start()

    def qsend(d, t, s):
        out, into, s_sem, r_sem = (sp, rp, qs_p, qr_p) if d > 0 else (sm, rm, qs_m, qr_m)
        return pltpu.make_async_remote_copy(
            src_ref=out.at[t - 1, s], dst_ref=into.at[t - 1, s],
            send_sem=s_sem.at[t - 1, s], recv_sem=r_sem.at[t - 1, s],
            device_id=(y, x, zrel(d), c), device_id_type=MESH,
        )

    def first_half(d):
        return (0, HALF) if d > 0 else (HALF, MOST)

    def has(d, t, s):
        return t > 1 or first_half(d)[0] <= s < first_half(d)[1]

    def qstep(d, t, s, add):
        out, into = (sp, rp) if d > 0 else (sm, rm)
        own = pp[s, c, zrel(d * (top + 1 - t))]
        if add:
            qsend(d, t - 1, s).wait_recv()
            own = (own.astype(F32) + into[t - 2, s].astype(F32)).astype(BF)
        out[t - 1, s] = own
        qsend(d, t, s).start()

    def added(s):
        pair_copy(s).wait_recv()

        @pl.loop(0, nz)
        def _(zz):
            pp[s, c, zz] = (pp[s, c, zz].astype(F32) + rr[s, zz].astype(F32)).astype(BF)

        for d in (1, -1):
            if has(d, 1, s):
                qstep(d, 1, s, False)
            elif top > 1:
                qstep(d, 2, s, False)

    def ysend(d, t, s):
        blk = yb.at[yrel(-d * (t - 1)), s]
        s_sem, r_sem = (ys_p, yr_p) if d > 0 else (ys_m, yr_m)
        return pltpu.make_async_remote_copy(
            src_ref=blk, dst_ref=blk, send_sem=s_sem.at[t - 1, s], recv_sem=r_sem.at[t - 1, s],
            device_id=(yrel(d), x, z, c), device_id_type=MESH,
        )

    def yhas(d, t, s):
        return t < ytop or first_half(d)[0] <= s < first_half(d)[1]

    def yrecv(d, t, s):
        blk = yb.at[yrel(-d * t), s]
        pltpu.make_async_copy(blk, blk, (yr_p if d > 0 else yr_m).at[t - 1, s]).wait()

    def done(s):
        total = pp[s, c, z].astype(F32)
        for d, into in ((1, rp), (-1, rm)):
            if has(d, top, s):
                qsend(d, top, s).wait_recv()
                total = total + into[top - 1, s].astype(F32)
        yb[y, s] = total.astype(BF)
        for d in (1, -1):
            if yhas(d, 1, s):
                ysend(d, 1, s).start()

    def ystep(t, s):
        for d in (1, -1):
            if yhas(d, t, s):
                yrecv(d, t, s)
                if t < ytop and yhas(d, t + 1, s):
                    ysend(d, t + 1, s).start()

    for s in range(MOST + 1):
        if s < MOST:
            partial(s)
        if s:
            added(s - 1)
    for t in range(2, top + 1):
        for s in range(MOST):
            for d in (1, -1):
                if t > 2 or has(d, 1, s):
                    qstep(d, t, s, True)
    for s in range(MOST):
        done(s)
    for t in range(1, ytop + 1):
        for s in range(MOST):
            ystep(t, s)

    def xcopy(i, m):
        to = xrel(i)
        part = pl.ds(m * PAIR_DEV, PAIR_DEV)
        return pltpu.make_async_remote_copy(
            src_ref=xs.at[to, part], dst_ref=(xr_d, xr_m)[m].at[x], send_sem=xs_s.at[m, i], recv_sem=xs_r.at[m, i],
            device_id=(y, to, z, c), device_id_type=MESH,
        )

    for m in (1, 0):
        for i in list(range(1, nx)) + [0]:
            to = xrel(i)
            for j in range(m * PAIR_DEV, (m + 1) * PAIR_DEV):
                got = yb[loc_t[to * 4 + j], loc_t[4 * nx + to * 4 + j]]
                if i:
                    xs[to, j] = got
                else:
                    (xr_d, xr_m)[m][to, j - m * PAIR_DEV] = got
            if i:
                xcopy(i, m).start()

    for f in fetch[3:]:
        f.wait()
    for i in range(1, nx):
        xcopy(i, 1).wait_recv()

    srows = xs.shape[2]
    at_r = lax.broadcasted_iota(jnp.int32, (srows, 128), 0)
    at_l = lax.broadcasted_iota(jnp.int32, (srows, 128), 1)

    def ordered(m, j, spread, mask):
        got = (xr_d, xr_m)[m][loc_t[8 * nx + x * 4 + m * PAIR_DEV + j], j].astype(F32)
        kept = [
            jnp.where((at_r < units * NB) & (at_l >= k * NB) & (at_l < (k + 1) * NB), got, 0.0).astype(BF)
            for k in range(CW)
        ]
        parts = []
        for k in range(CW):
            wide = jnp.dot(kept[k], spread[...], preferred_element_type=F32)
            parts.append((wide * mask[...].astype(F32)).astype(BF))
        return jnp.dot(collect[...], jnp.concatenate(parts, axis=0), preferred_element_type=F32)

    rpad = up(share, 32)
    turned = jnp.concatenate(
        [ordered(1, j, spread_m, mask_m) for j in range(PAIR_DEV)]
        + [jnp.zeros((128 - PAIR_DEV * rpad, rows * rpad), F32)], axis=0,
    ).T.astype(BF)
    for r in range(rows):
        ms[r] = turned[r * rpad:(r + 1) * rpad, :]
    mr[row] = ms[row]

    def mcopy(i):
        to = lax.rem(row + i, rows)
        return pltpu.make_async_remote_copy(
            src_ref=ms.at[to], dst_ref=mr.at[row], send_sem=ms_s.at[i], recv_sem=ms_r.at[i],
            device_id=at_row(to), device_id_type=MESH,
        )

    @pl.loop(1, rows)
    def _(i):
        mcopy(i).start()

    for i in range(1, nx):
        xcopy(i, 0).wait_recv()
    for j in range(PAIR_DEV):
        out_d[j] = ordered(0, j, spread_d, mask_d)[:share, :NB * NB].astype(BF)

    @pl.loop(1, rows)
    def _(i):
        mcopy(i).wait_recv()

    for j in range(PAIR_DEV):
        out_m[j] = jnp.concatenate(
            [mr[r].astype(F32)[:share, j * rpad:j * rpad + share] for r in range(rows)], axis=1
        ).astype(BF)

    for n in range(2):
        for i in range(ny):
            if i:
                by(n, i).wait_send()
            for k in range(1, nx):
                bx(n, i, k).wait_send()
    for t in range(1, top + 1):
        for h in range(CHUNKS):
            for d in (1, -1):
                if g_has(d, t, h):
                    gsend(d, t, h).wait_send()
    for k in range(nz):
        for h in range(2):
            sibling(k, c, h).wait_send()
    for s in range(MOST):
        pair_copy(s).wait_send()
        for t in range(1, top + 1):
            for d in (1, -1):
                if has(d, t, s):
                    qsend(d, t, s).wait_send()
        for t in range(1, ytop + 1):
            for d in (1, -1):
                if yhas(d, t, s):
                    ysend(d, t, s).wait_send()
    for m in range(2):
        for i in range(1, nx):
            xcopy(i, m).wait_send()

    @pl.loop(1, rows)
    def _(i):
        mcopy(i).wait_send()


def constants(rows):
    share = NB * NB // rows
    units = NB * CG // rows
    srows = up(units * NB, 16)
    rpad = up(share, 32)
    lane = np.arange(128)
    plain = np.arange(up(NB * NB, 128))
    wd = np.where(plain < NB * NB, plain, -1)
    padded = np.arange(rows * rpad)
    wdm = np.where(padded % rpad < share, padded // rpad * share + padded % rpad, -1)
    r = np.arange(srows)

    def two(cols):
        spread = (lane[:, None] < CW * NB) & (cols[None, :] >= 0) & (lane[:, None] % NB == cols[None, :] % NB)
        mask = (r[:, None] < units * NB) & (cols[None, :] >= 0) & (r[:, None] % NB == cols[None, :] // NB)
        return spread, mask

    k = np.arange(CW * srows)
    out = np.arange(rpad)
    rr = k % srows
    collect = (
        (rr[None, :] < units * NB) & (out[:, None] < share)
        & (rr[None, :] // NB == out[:, None] // CW) & (k[None, :] // srows == out[:, None] % CW)
    )
    return [a.astype(np.float32).astype(BF) for a in (*two(wd), *two(wdm), collect)]


def solution(mesh):
    sizes = tuple(int(np.prod([mesh.shape[a]])) for a in ("pb", "row"))
    nx, ny, nz = GRID.get(sizes, (4, 8, 8))
    split = Mesh(mesh.devices.reshape(ny, nx, nz, 2), ("y", "x", "z", "c"))
    npb, rows = ny * nx, 2 * nz
    share, units = NB * NB // rows, NB * CG // rows
    srows, rpad = up(units * NB, 16), up(share, 32)
    top, ytop = nz // 2, ny // 2
    dma = pltpu.SemaphoreType.DMA

    def shards(val, con, screened, pair_list, transfer_index, owner_map):
        pairs = pair_list.shape[0]
        tab = jnp.concatenate([transfer_index[:, 0], pair_list[:, 0], pair_list[:, 1], owner_map])
        consts = [jnp.asarray(a) for a in constants(rows)]
        vmem, anywhere = pl.BlockSpec(memory_space=pltpu.VMEM), pl.BlockSpec(memory_space=pl.ANY)
        points = screened.shape[2]
        blk = (srows, 128)
        scratch = [
            pltpu.VMEM(val.shape, BF), pltpu.VMEM(con.shape, BF),
            pltpu.VMEM((256, points), BF),
            *[pltpu.VMEM(a.shape, BF) for a in consts],
            pltpu.VMEM((ny, nx, KB, 128), BF),
            pltpu.VMEM((ny, nx, KB, 128), BF),
            pltpu.VMEM((rows, 2 * MOST, KB, 128), BF),
            pltpu.VMEM((MOST, NB * BP, 256), F32),
            pltpu.VMEM((NB * BP, 512), BF),
            pltpu.VMEM((NB * BP, 256), BF),
            pltpu.VMEM((rows, *blk), F32),
            pltpu.VMEM((MOST, 2, nz, *blk), BF),
            pltpu.VMEM((MOST, nz, *blk), BF),
            *[pltpu.VMEM((top, MOST, *blk), BF) for _ in range(4)],
            pltpu.VMEM((ny, MOST, *blk), BF),
            pltpu.VMEM((nx, 2 * PAIR_DEV, *blk), BF),
            pltpu.VMEM((nx, PAIR_DEV, *blk), BF),
            pltpu.VMEM((nx, PAIR_DEV, *blk), BF),
            pltpu.VMEM((rows, rpad, 128), BF),
            pltpu.VMEM((rows, rpad, 128), BF),
            pltpu.SMEM((12 * nx,), jnp.int32),
            dma((8,)),
            dma((2, ny)), dma((2, ny)), dma((2, ny, nx)), dma((2, ny, nx)),
            *[dma((top, CHUNKS)) for _ in range(4)],
            dma((nz, 2)), dma((nz, 2)),
            dma((MOST,)), dma((MOST,)),
            *[dma((top, MOST)) for _ in range(4)],
            *[dma((ytop, MOST)) for _ in range(4)],
            dma((2, nx)), dma((2, nx)), dma((rows,)), dma((rows,)),
        ]
        result = jax.ShapeDtypeStruct((PAIR_DEV, share, NB * NB), BF)
        return pl.pallas_call(
            functools.partial(kernel, ny, nx, nz, pairs),
            out_shape=(result, result),
            in_specs=[pl.BlockSpec(memory_space=pltpu.SMEM), *[anywhere] * 8],
            out_specs=(vmem, vmem),
            scratch_shapes=scratch,
            compiler_params=pltpu.CompilerParams(
                collective_id=0, has_side_effects=True, vmem_limit_bytes=60 * 2**20
            ),
        )(tab, val, con, screened, *consts)

    in_specs = (P(("y", "x"), None, ("z", "c")), P(("y", "x"), None, ("z", "c")),
                P(("y", "x"), ("z", "c"), None), P(), P(), P())
    out = P(("y", "x"), ("z", "c"), None)
    return jax.shard_map(shards, mesh=split, in_specs=in_specs, out_specs=(out, out), check_vma=False)


GRID = {(4, 4): (2, 2, 2), (2, 8): (1, 2, 4)}
```

```python
import functools

import jax
import jax.numpy as jnp
import numpy as np
from jax import lax
from jax.experimental import pallas as pl
from jax.experimental.pallas import tpu as pltpu
from jax.sharding import Mesh
from jax.sharding import PartitionSpec as P

MESH = pl.DeviceIdType.MESH
BF = jnp.bfloat16
F32 = jnp.float32
NB = 20
BP = 24
KB = 2 * BP
CG = 4
CW = NB // CG
WIDE = CW * NB
TAIL = WIDE // CG
PAIR_DEV = 2
MOST = 6
HALF = MOST // 2
CHUNKS = 4


def up(n, to):
    return -(-n // to) * to


def kernel(
    ny, nx, nz, pairs,
    tq, tp, to_slot, val_any, con_any, w_any, spread_d_any, mask_d_any, spread_m_any, mask_m_any, collect_any,
    out_d, out_m,
    val, con, w, spread_d, mask_d, spread_m, mask_m, collect,
    call, vall, g, acc, prod, valp, pf, pp, rr, rp, rm, sp, sm, yb, xs, xr_d, xr_m, ms, mr,
    loc_t, loc,
    by_s, by_r, bx_s, bx_r,
    gs_p, gr_p, gs_m, gr_m, ss_s, ss_r,
    p_s, p_r, qs_p, qr_p, qs_m, qr_m,
    ys_p, yr_p, ys_m, yr_m, xs_s, xs_r, ms_s, ms_r,
):
    y, x, z, c = (lax.axis_index(a) for a in ("y", "x", "z", "c"))
    rows = 2 * nz
    me = y * nx + x
    row = z * 2 + c
    share = NB * NB // rows
    units = NB * CG // rows
    top, ytop = nz // 2, ny // 2

    def at_row(r):
        return (y, x, r // 2, lax.rem(r, 2))

    def zrel(k):
        return lax.rem(z + k + 2 * nz, nz)

    def yrel(k):
        return lax.rem(y + k + 2 * ny, ny)

    def xrel(k):
        return lax.rem(x + k + 2 * nx, nx)

    barrier = pltpu.get_barrier_semaphore()
    for i in range(1, nx):
        pl.semaphore_signal(barrier, inc=1, device_id=(y, xrel(i), z, c), device_id_type=MESH)
    for i in range(1, ny):
        pl.semaphore_signal(barrier, inc=1, device_id=(yrel(i), x, z, c), device_id_type=MESH)

    @pl.loop(1, rows)
    def _(i):
        pl.semaphore_signal(barrier, inc=1, device_id=at_row(lax.rem(row + i, rows)), device_id_type=MESH)

    fetch = [
        pltpu.make_async_copy(a, b, loc.at[i])
        for i, (a, b) in enumerate((
            (con_any, con), (val_any, val), (w_any.at[0], w), (spread_d_any, spread_d), (mask_d_any, mask_d),
            (spread_m_any, spread_m), (mask_m_any, mask_m), (collect_any, collect),
        ))
    ]
    for f in fetch:
        f.start()

    def stage(buf, src):
        blank = jnp.zeros((BP - NB, 128), BF)
        for h in range(2):
            part = src[0, :, h * 128:(h + 1) * 128]
            buf[y, x, h * BP:(h + 1) * BP, :] = jnp.concatenate([part, blank], axis=0)

    fetch[0].wait()
    stage(call, con)
    fetch[1].wait()
    stage(vall, val)
    pl.semaphore_wait(barrier, nx - 1 + ny - 1 + rows - 1)

    near = sorted(range(1, ny), key=lambda i: min(i, ny - i))

    def by(n, i):
        ref = (call, vall)[n].at[y, x]
        return pltpu.make_async_remote_copy(
            src_ref=ref, dst_ref=ref, send_sem=by_s.at[n, i], recv_sem=by_r.at[n, i],
            device_id=(yrel(i), x, z, c), device_id_type=MESH,
        )

    def bx(n, i, k):
        ref = (call, vall)[n].at[yrel(-i), x]
        return pltpu.make_async_remote_copy(
            src_ref=ref, dst_ref=ref, send_sem=bx_s.at[n, i, k], recv_sem=bx_r.at[n, i, k],
            device_id=(y, xrel(k), z, c), device_id_type=MESH,
        )

    def b_arrived(n, i, k):
        ref = (call, vall)[n].at[yrel(-i), xrel(-k)]
        pltpu.make_async_copy(ref, ref, bx_r.at[n, i, k] if k else by_r.at[n, i]).wait()

    def pass_on(n, i):
        if i:
            b_arrived(n, i, 0)
        for k in range(1, nx):
            bx(n, i, k).start()

    def all_arrived(n):
        for i in [0] + near:
            for k in range(1, nx):
                b_arrived(n, i, k)

    pass_on(0, 0)
    for n in range(2):
        for i in near:
            by(n, i).start()

    pf[...] = jnp.zeros(pf.shape, F32)

    @pl.loop(0, MOST)
    def _(s):
        acc[s] = jnp.zeros(acc.shape[1:], F32)

    for i in near:
        pass_on(0, i)

    def owner(k):
        return to_slot[k]

    def own_slots(p, carry):
        count, slots = carry
        hit = tq[0, p] == me
        slots = tuple(jnp.where(hit & (count == s), p, slots[s]) for s in range(MOST))
        return count + hit.astype(jnp.int32), slots

    zero = jnp.int32(0)
    _, slots = lax.fori_loop(0, pairs, own_slots, (zero, (zero,) * MOST))
    first = [owner(tp[0, p]) for p in slots]
    second = [owner(tp[1, p]) for p in slots]

    def by_second(p, carry):
        e = owner(tp[1, p])
        new = []
        for k in range(nx):
            count, one, two = carry[k]
            hit = e == y * nx + k
            new.append((count + hit.astype(jnp.int32), jnp.where(hit & (count == 0), p, one),
                        jnp.where(hit & (count == 1), p, two)))
        return tuple(new)

    found = lax.fori_loop(0, pairs, by_second, ((zero,) * 3,) * nx)
    wanted = []
    for k in range(nx):
        at = (y * nx + k) * PAIR_DEV
        wanted += [at, at + 1, found[k][1], found[k][2]]
    column = [tq[0, p] for p in wanted]

    def ranks(p, carry):
        return tuple(
            n + ((tq[0, p] == q) & (p < own)).astype(jnp.int32) for n, q, own in zip(carry, column, wanted)
        )

    ranked = lax.fori_loop(0, pairs, ranks, (zero,) * len(wanted))
    for i in range(4 * nx):
        loc_t[i] = lax.div(column[i], nx)
        loc_t[4 * nx + i] = jnp.minimum(ranked[i], MOST - 1)
        loc_t[8 * nx + i] = lax.rem(column[i], nx)

    for i in [0] + near:
        pass_on(1, i)
    all_arrived(0)

    for i, k in enumerate(first + second):
        g[row, i] = call[lax.div(k, nx), lax.rem(k, nx)]

    def g_has(d, t, h):
        return t < top or (h < CHUNKS // 2) == (d > 0)

    def g_ref(k, h):
        return g.at[zrel(k) * 2 + c, pl.ds(h * (2 * MOST // CHUNKS), 2 * MOST // CHUNKS)]

    def gsend(d, t, h):
        ref = g_ref(-d * (t - 1), h)
        s_sem, r_sem = (gs_p, gr_p) if d > 0 else (gs_m, gr_m)
        return pltpu.make_async_remote_copy(
            src_ref=ref, dst_ref=ref, send_sem=s_sem.at[t - 1, h], recv_sem=r_sem.at[t - 1, h],
            device_id=(y, x, zrel(d), c), device_id_type=MESH,
        )

    def grecv(d, t, h):
        ref = g_ref(-d * t, h)
        pltpu.make_async_copy(ref, ref, (gr_p if d > 0 else gr_m).at[t - 1, h]).wait()

    def sibling(zz, core, h):
        ref = g.at[zz * 2 + core, pl.ds(h * MOST, MOST)]
        return pltpu.make_async_remote_copy(
            src_ref=ref, dst_ref=ref, send_sem=ss_s.at[zz, h], recv_sem=ss_r.at[zz, h],
            device_id=(y, x, z, 1 - c), device_id_type=MESH,
        )

    def block_slot(zz, s):
        for core in range(2):
            for h in range(2):
                lane = (core * 2 + h) * 128
                one = g[zz * 2 + core, s, h * BP:(h + 1) * BP, :]
                two = g[zz * 2 + core, MOST + s, h * BP:(h + 1) * BP, :]
                for k in range(NB):
                    prod[k * BP:(k + 1) * BP, lane:lane + 128] = one[k:k + 1, :] * two
        cols = pl.ds(pl.multiple_of(zz * 512, 512), 512)
        acc[s] += lax.dot_general(
            prod[...], w[:, cols], (((1,), (1,)), ((), ())), preferred_element_type=F32
        )

    def block_in(zz):
        for h in range(2):
            sibling(zz, 1 - c, h).wait_recv()

    def block(zz):
        block_in(zz)

        @pl.loop(0, MOST)
        def _(s):
            block_slot(zz, s)

    for h in range(CHUNKS):
        for d in (1, -1):
            if g_has(d, 1, h):
                gsend(d, 1, h).start()
    for h in range(2):
        sibling(z, c, h).start()
    fetch[2].wait()
    before = [z]
    for t in range(1, top + 1):
        for h in range(CHUNKS):
            for d in (1, -1):
                if g_has(d, t, h):
                    grecv(d, t, h)
                    if t < top and g_has(d, t + 1, h):
                        gsend(d, t + 1, h).start()
            if (h + 1) % (CHUNKS // 2) == 0:
                half = (h + 1) // (CHUNKS // 2) - 1
                for d in (1, -1):
                    if g_has(d, t, h):
                        sibling(zrel(-d * t), c, half).start()
                if half < len(before):
                    block(before[half])
        before = [zrel(-t), zrel(t)] if t < top else [zrel(t)]
    all_arrived(1)

    def pair_copy(s):
        return pltpu.make_async_remote_copy(
            src_ref=pp.at[s, 1 - c], dst_ref=rr.at[s], send_sem=p_s.at[s], recv_sem=p_r.at[s],
            device_id=(y, x, z, 1 - c), device_id_type=MESH,
        )

    def partial(s):
        one = vall[lax.div(first[s], nx), lax.rem(first[s], nx)]
        two = vall[lax.div(second[s], nx), lax.rem(second[s], nx)]
        for h in range(2):
            a, b = one[h * BP:(h + 1) * BP, :], two[h * BP:(h + 1) * BP, :]
            for k in range(NB):
                valp[k * BP:(k + 1) * BP, h * 128:(h + 1) * 128] = a[k:k + 1, :] * b
        for q in range(CG):
            it = jnp.concatenate(
                [acc[s, (q * CW + k) * BP:(q * CW + k) * BP + NB, :] for k in range(CW)]
                + [jnp.zeros((128 - CW * NB, 256), F32)], axis=0,
            ).astype(BF)
            part = lax.dot_general(valp[...], it, (((1,), (1,)), ((), ())), preferred_element_type=F32)
            for v in range(NB):
                u = v * CG + q
                r, i = u // units, u % units
                piece = part[v * BP:(v + 1) * BP, :]
                if i < CG:
                    pf[r, i * NB:(i + 1) * NB, :WIDE] = piece[:NB, :WIDE]
                else:
                    for k in range(CG):
                        moved = pltpu.roll(piece, WIDE - k * TAIL, 1)
                        pf[r, k * NB:(k + 1) * NB, WIDE:WIDE + TAIL] = moved[:NB, WIDE:WIDE + TAIL]
        for r in range(rows):
            pp[s, r % 2, r // 2] = pf[r].astype(BF)
        pair_copy(s).start()

    def qsend(d, t, s):
        out, into, s_sem, r_sem = (sp, rp, qs_p, qr_p) if d > 0 else (sm, rm, qs_m, qr_m)
        return pltpu.make_async_remote_copy(
            src_ref=out.at[t - 1, s], dst_ref=into.at[t - 1, s],
            send_sem=s_sem.at[t - 1, s], recv_sem=r_sem.at[t - 1, s],
            device_id=(y, x, zrel(d), c), device_id_type=MESH,
        )

    def first_half(d):
        return (0, HALF) if d > 0 else (HALF, MOST)

    def has(d, t, s):
        return t > 1 or first_half(d)[0] <= s < first_half(d)[1]

    def qstep(d, t, s, add):
        out, into = (sp, rp) if d > 0 else (sm, rm)
        own = pp[s, c, zrel(d * (top + 1 - t))]
        if add:
            qsend(d, t - 1, s).wait_recv()
            own = (own.astype(F32) + into[t - 2, s].astype(F32)).astype(BF)
        out[t - 1, s] = own
        qsend(d, t, s).start()

    def added(s):
        pair_copy(s).wait_recv()

        @pl.loop(0, nz)
        def _(zz):
            pp[s, c, zz] = (pp[s, c, zz].astype(F32) + rr[s, zz].astype(F32)).astype(BF)

        for d in (1, -1):
            if has(d, 1, s):
                qstep(d, 1, s, False)
            elif top > 1:
                qstep(d, 2, s, False)

    def ysend(d, t, s):
        blk = yb.at[yrel(-d * (t - 1)), s]
        s_sem, r_sem = (ys_p, yr_p) if d > 0 else (ys_m, yr_m)
        return pltpu.make_async_remote_copy(
            src_ref=blk, dst_ref=blk, send_sem=s_sem.at[t - 1, s], recv_sem=r_sem.at[t - 1, s],
            device_id=(yrel(d), x, z, c), device_id_type=MESH,
        )

    def yhas(d, t, s):
        return t < ytop or first_half(d)[0] <= s < first_half(d)[1]

    def yrecv(d, t, s):
        blk = yb.at[yrel(-d * t), s]
        pltpu.make_async_copy(blk, blk, (yr_p if d > 0 else yr_m).at[t - 1, s]).wait()

    def done(s):
        total = pp[s, c, z].astype(F32)
        for d, into in ((1, rp), (-1, rm)):
            if has(d, top, s):
                qsend(d, top, s).wait_recv()
                total = total + into[top - 1, s].astype(F32)
        yb[y, s] = total.astype(BF)
        for d in (1, -1):
            if yhas(d, 1, s):
                ysend(d, 1, s).start()

    def ystep(t, s):
        for d in (1, -1):
            if yhas(d, t, s):
                yrecv(d, t, s)
                if t < ytop and yhas(d, t + 1, s):
                    ysend(d, t + 1, s).start()

    for s in range(MOST + 1):
        if s == 0:
            for zz in before:
                block_in(zz)
        if s < MOST:
            for zz in before:
                block_slot(zz, s)
            partial(s)
        if s:
            added(s - 1)
    for t in range(2, top + 1):
        for s in range(MOST):
            for d in (1, -1):
                if t > 2 or has(d, 1, s):
                    qstep(d, t, s, True)
    for s in range(MOST):
        done(s)
    for t in range(1, ytop + 1):
        for s in range(MOST):
            ystep(t, s)

    def xcopy(i, m):
        to = xrel(i)
        part = pl.ds(m * PAIR_DEV, PAIR_DEV)
        return pltpu.make_async_remote_copy(
            src_ref=xs.at[to, part], dst_ref=(xr_d, xr_m)[m].at[x], send_sem=xs_s.at[m, i], recv_sem=xs_r.at[m, i],
            device_id=(y, to, z, c), device_id_type=MESH,
        )

    for m in (1, 0):
        for i in list(range(1, nx)) + [0]:
            to = xrel(i)
            for j in range(m * PAIR_DEV, (m + 1) * PAIR_DEV):
                got = yb[loc_t[to * 4 + j], loc_t[4 * nx + to * 4 + j]]
                if i:
                    xs[to, j] = got
                else:
                    (xr_d, xr_m)[m][to, j - m * PAIR_DEV] = got
            if i:
                xcopy(i, m).start()

    for f in fetch[3:]:
        f.wait()
    for i in range(1, nx):
        xcopy(i, 1).wait_recv()

    srows = mask_d.shape[0]
    at_r = lax.broadcasted_iota(jnp.int32, (srows, 128), 0)
    at_l = lax.broadcasted_iota(jnp.int32, (srows, 128), 1)

    def ordered(m, j, spread, mask):
        base = (xr_d, xr_m)[m][loc_t[8 * nx + x * 4 + m * PAIR_DEV + j], j].astype(F32)
        last = jnp.zeros((NB, 128), F32)
        lane = lax.broadcasted_iota(jnp.int32, (NB, 128), 1)
        for k in range(CG):
            moved = pltpu.roll(base[k * NB:(k + 1) * NB, :], 128 - (WIDE - k * TAIL), 1)
            last = jnp.where((lane >= k * TAIL) & (lane < (k + 1) * TAIL), moved, last)
        got = jnp.concatenate([base, last, jnp.zeros((srows - units * NB, 128), F32)], axis=0)
        kept = [
            jnp.where((at_r < units * NB) & (at_l >= k * NB) & (at_l < (k + 1) * NB), got, 0.0).astype(BF)
            for k in range(CW)
        ]
        parts = []
        for k in range(CW):
            wide = jnp.dot(kept[k], spread[...], preferred_element_type=F32)
            parts.append((wide * mask[...].astype(F32)).astype(BF))
        return jnp.dot(collect[...], jnp.concatenate(parts, axis=0), preferred_element_type=F32)

    rpad = up(share, 32)
    turned = jnp.concatenate(
        [ordered(1, j, spread_m, mask_m) for j in range(PAIR_DEV)]
        + [jnp.zeros((128 - PAIR_DEV * rpad, rows * rpad), F32)], axis=0,
    ).T.astype(BF)
    for r in range(rows):
        ms[r] = turned[r * rpad:(r + 1) * rpad, :]
    mr[row] = ms[row]

    def mcopy(i):
        to = lax.rem(row + i, rows)
        return pltpu.make_async_remote_copy(
            src_ref=ms.at[to], dst_ref=mr.at[row], send_sem=ms_s.at[i], recv_sem=ms_r.at[i],
            device_id=at_row(to), device_id_type=MESH,
        )

    @pl.loop(1, rows)
    def _(i):
        mcopy(i).start()

    for i in range(1, nx):
        xcopy(i, 0).wait_recv()
    out_d[...] = jnp.stack(
        [ordered(0, j, spread_d, mask_d)[:share, :NB * NB] for j in range(PAIR_DEV)], axis=1
    ).astype(BF)

    @pl.loop(1, rows)
    def _(i):
        mcopy(i).wait_recv()

    out_m[...] = jnp.stack([
        jnp.concatenate(
            [mr[r].astype(F32)[:share, j * rpad:j * rpad + share] for r in range(rows)], axis=1
        ) for j in range(PAIR_DEV)
    ], axis=1).astype(BF)

    for n in range(2):
        for i in range(ny):
            if i:
                by(n, i).wait_send()
            for k in range(1, nx):
                bx(n, i, k).wait_send()
    for t in range(1, top + 1):
        for h in range(CHUNKS):
            for d in (1, -1):
                if g_has(d, t, h):
                    gsend(d, t, h).wait_send()
    for k in range(nz):
        for h in range(2):
            sibling(k, c, h).wait_send()
    for s in range(MOST):
        pair_copy(s).wait_send()
        for t in range(1, top + 1):
            for d in (1, -1):
                if has(d, t, s):
                    qsend(d, t, s).wait_send()
        for t in range(1, ytop + 1):
            for d in (1, -1):
                if yhas(d, t, s):
                    ysend(d, t, s).wait_send()
    for m in range(2):
        for i in range(1, nx):
            xcopy(i, m).wait_send()

    @pl.loop(1, rows)
    def _(i):
        mcopy(i).wait_send()


def constants(rows):
    share = NB * NB // rows
    units = NB * CG // rows
    srows = up(units * NB, 16)
    rpad = up(share, 32)
    lane = np.arange(128)
    plain = np.arange(up(NB * NB, 128))
    wd = np.where(plain < NB * NB, plain, -1)
    padded = np.arange(rows * rpad)
    wdm = np.where(padded % rpad < share, padded // rpad * share + padded % rpad, -1)
    r = np.arange(srows)

    def two(cols):
        spread = (lane[:, None] < CW * NB) & (cols[None, :] >= 0) & (lane[:, None] % NB == cols[None, :] % NB)
        mask = (r[:, None] < units * NB) & (cols[None, :] >= 0) & (r[:, None] % NB == cols[None, :] // NB)
        return spread, mask

    k = np.arange(CW * srows)
    out = np.arange(rpad)
    rr = k % srows
    collect = (
        (rr[None, :] < units * NB) & (out[:, None] < share)
        & (rr[None, :] // NB == out[:, None] // CW) & (k[None, :] // srows == out[:, None] % CW)
    )
    return [a.astype(np.float32).astype(BF) for a in (*two(wd), *two(wdm), collect)]


def solution(mesh):
    sizes = tuple(int(np.prod([mesh.shape[a]])) for a in ("pb", "row"))
    nx, ny, nz = GRID.get(sizes, (4, 8, 8))
    split = Mesh(mesh.devices.reshape(ny, nx, nz, 2), ("y", "x", "z", "c"))
    npb, rows = ny * nx, 2 * nz
    share, units = NB * NB // rows, NB * CG // rows
    srows, rpad = up(units * NB, 16), up(share, 32)
    top, ytop = nz // 2, ny // 2
    dma = pltpu.SemaphoreType.DMA

    def shards(val, con, screened, pair_list, transfer_index, owner_map):
        pairs = pair_list.shape[0]
        consts = [jnp.asarray(a) for a in constants(rows)]
        vmem, anywhere = pl.BlockSpec(memory_space=pltpu.VMEM), pl.BlockSpec(memory_space=pl.ANY)
        points = screened.shape[2]
        blk = ((units - 1) * NB, 128)
        scratch = [
            pltpu.VMEM(val.shape, BF), pltpu.VMEM(con.shape, BF),
            pltpu.VMEM((256, points), BF),
            *[pltpu.VMEM(a.shape, BF) for a in consts],
            pltpu.VMEM((ny, nx, KB, 128), BF),
            pltpu.VMEM((ny, nx, KB, 128), BF),
            pltpu.VMEM((rows, 2 * MOST, KB, 128), BF),
            pltpu.VMEM((MOST, NB * BP, 256), F32),
            pltpu.VMEM((NB * BP, 512), BF),
            pltpu.VMEM((NB * BP, 256), BF),
            pltpu.VMEM((rows, *blk), F32),
            pltpu.VMEM((MOST, 2, nz, *blk), BF),
            pltpu.VMEM((MOST, nz, *blk), BF),
            *[pltpu.VMEM((top, MOST, *blk), BF) for _ in range(4)],
            pltpu.VMEM((ny, MOST, *blk), BF),
            pltpu.VMEM((nx, 2 * PAIR_DEV, *blk), BF),
            pltpu.VMEM((nx, PAIR_DEV, *blk), BF),
            pltpu.VMEM((nx, PAIR_DEV, *blk), BF),
            pltpu.VMEM((rows, rpad, 128), BF),
            pltpu.VMEM((rows, rpad, 128), BF),
            pltpu.SMEM((12 * nx,), jnp.int32),
            dma((8,)),
            dma((2, ny)), dma((2, ny)), dma((2, ny, nx)), dma((2, ny, nx)),
            *[dma((top, CHUNKS)) for _ in range(4)],
            dma((nz, 2)), dma((nz, 2)),
            dma((MOST,)), dma((MOST,)),
            *[dma((top, MOST)) for _ in range(4)],
            *[dma((ytop, MOST)) for _ in range(4)],
            dma((2, nx)), dma((2, nx)), dma((rows,)), dma((rows,)),
        ]
        result = jax.ShapeDtypeStruct((share, PAIR_DEV, NB * NB), BF)
        direct, mirror = pl.pallas_call(
            functools.partial(kernel, ny, nx, nz, pairs),
            out_shape=(result, result),
            in_specs=[*[pl.BlockSpec(memory_space=pltpu.SMEM)] * 3, *[anywhere] * 8],
            out_specs=(vmem, vmem),
            scratch_shapes=scratch,
            compiler_params=pltpu.CompilerParams(
                collective_id=0, has_side_effects=True, vmem_limit_bytes=60 * 2**20
            ),
        )(transfer_index.T, pair_list.T, owner_map, val, con, screened, *consts)
        return direct.transpose(1, 0, 2), mirror.transpose(1, 0, 2)

    in_specs = (P(("y", "x"), None, ("z", "c")), P(("y", "x"), None, ("z", "c")),
                P(("y", "x"), ("z", "c"), None), P(), P(), P())
    out = P(("y", "x"), ("z", "c"), None)
    return jax.shard_map(shards, mesh=split, in_specs=in_specs, out_specs=(out, out), check_vma=False)


GRID = {(4, 4): (2, 2, 2), (2, 8): (1, 2, 4)}
```

```python
import functools

import jax
import jax.numpy as jnp
import numpy as np
from jax import lax
from jax.experimental import pallas as pl
from jax.experimental.pallas import tpu as pltpu
from jax.sharding import Mesh
from jax.sharding import PartitionSpec as P

MESH = pl.DeviceIdType.MESH
BF = jnp.bfloat16
F32 = jnp.float32
NB = 20
BP = 24
KB = 2 * BP
CG = 4
CW = NB // CG
WIDE = CW * NB
TAIL = WIDE // CG
PAIR_DEV = 2
MOST = 6
HALF = MOST // 2
CHUNKS = 4


def up(n, to):
    return -(-n // to) * to


def kernel(
    ny, nx, nz, pairs,
    tq, tp, to_slot, val_any, con_any, w_any, spread_d_any, mask_d_any, spread_m_any, mask_m_any, collect_any,
    out_d, out_m,
    val, con, w, spread_d, mask_d, spread_m, mask_m, collect,
    wt, call, vall, g, acc, prod, valp, pf, pp, rr, rp, rm, sp, sm, yb, xs, xr_d, xr_m, ms, mr,
    loc_t, loc,
    by_s, by_r, bx_s, bx_r,
    gs_p, gr_p, gs_m, gr_m, ss_s, ss_r,
    p_s, p_r, qs_p, qr_p, qs_m, qr_m,
    ys_p, yr_p, ys_m, yr_m, xs_s, xs_r, ms_s, ms_r,
):
    y, x, z, c = (lax.axis_index(a) for a in ("y", "x", "z", "c"))
    rows = 2 * nz
    me = y * nx + x
    row = z * 2 + c
    share = NB * NB // rows
    units = NB * CG // rows
    top, ytop = nz // 2, ny // 2

    def at_row(r):
        return (y, x, r // 2, lax.rem(r, 2))

    def zrel(k):
        return lax.rem(z + k + 2 * nz, nz)

    def yrel(k):
        return lax.rem(y + k + 2 * ny, ny)

    def xrel(k):
        return lax.rem(x + k + 2 * nx, nx)

    barrier = pltpu.get_barrier_semaphore()
    for i in range(1, nx):
        pl.semaphore_signal(barrier, inc=1, device_id=(y, xrel(i), z, c), device_id_type=MESH)
    for i in range(1, ny):
        pl.semaphore_signal(barrier, inc=1, device_id=(yrel(i), x, z, c), device_id_type=MESH)

    @pl.loop(1, rows)
    def _(i):
        pl.semaphore_signal(barrier, inc=1, device_id=at_row(lax.rem(row + i, rows)), device_id_type=MESH)

    fetch = [
        pltpu.make_async_copy(a, b, loc.at[i])
        for i, (a, b) in enumerate((
            (con_any, con), (val_any, val), (w_any.at[0], w), (spread_d_any, spread_d), (mask_d_any, mask_d),
            (spread_m_any, spread_m), (mask_m_any, mask_m), (collect_any, collect),
        ))
    ]
    for f in fetch:
        f.start()

    def stage(buf, src):
        blank = jnp.zeros((BP - NB, 128), BF)
        for h in range(2):
            part = src[0, :, h * 128:(h + 1) * 128]
            buf[y, x, h * BP:(h + 1) * BP, :] = jnp.concatenate([part, blank], axis=0)

    fetch[0].wait()
    stage(call, con)
    fetch[1].wait()
    stage(vall, val)
    pl.semaphore_wait(barrier, nx - 1 + ny - 1 + rows - 1)

    near = sorted(range(1, ny), key=lambda i: min(i, ny - i))

    def by(n, i):
        ref = (call, vall)[n].at[y, x]
        return pltpu.make_async_remote_copy(
            src_ref=ref, dst_ref=ref, send_sem=by_s.at[n, i], recv_sem=by_r.at[n, i],
            device_id=(yrel(i), x, z, c), device_id_type=MESH,
        )

    def bx(n, i, k):
        ref = (call, vall)[n].at[yrel(-i), x]
        return pltpu.make_async_remote_copy(
            src_ref=ref, dst_ref=ref, send_sem=bx_s.at[n, i, k], recv_sem=bx_r.at[n, i, k],
            device_id=(y, xrel(k), z, c), device_id_type=MESH,
        )

    def b_arrived(n, i, k):
        ref = (call, vall)[n].at[yrel(-i), xrel(-k)]
        pltpu.make_async_copy(ref, ref, bx_r.at[n, i, k] if k else by_r.at[n, i]).wait()

    def pass_on(n, i):
        if i:
            b_arrived(n, i, 0)
        for k in range(1, nx):
            bx(n, i, k).start()

    def all_arrived(n):
        for i in [0] + near:
            for k in range(1, nx):
                b_arrived(n, i, k)

    pass_on(0, 0)
    for n in range(2):
        for i in near:
            by(n, i).start()

    pf[...] = jnp.zeros(pf.shape, F32)

    @pl.loop(0, MOST)
    def _(s):
        acc[s] = jnp.zeros(acc.shape[1:], F32)

    for i in near:
        pass_on(0, i)

    fetch[2].wait()
    for zz in range(nz):
        wt[zz] = w[:, zz * 512:(zz + 1) * 512].T

    def owner(k):
        return to_slot[k]

    def own_slots(p, carry):
        count, slots = carry
        hit = tq[0, p] == me
        slots = tuple(jnp.where(hit & (count == s), p, slots[s]) for s in range(MOST))
        return count + hit.astype(jnp.int32), slots

    zero = jnp.int32(0)
    _, slots = lax.fori_loop(0, pairs, own_slots, (zero, (zero,) * MOST))
    first = [owner(tp[0, p]) for p in slots]
    second = [owner(tp[1, p]) for p in slots]

    def by_second(p, carry):
        e = owner(tp[1, p])
        new = []
        for k in range(nx):
            count, one, two = carry[k]
            hit = e == y * nx + k
            new.append((count + hit.astype(jnp.int32), jnp.where(hit & (count == 0), p, one),
                        jnp.where(hit & (count == 1), p, two)))
        return tuple(new)

    found = lax.fori_loop(0, pairs, by_second, ((zero,) * 3,) * nx)
    wanted = []
    for k in range(nx):
        at = (y * nx + k) * PAIR_DEV
        wanted += [at, at + 1, found[k][1], found[k][2]]
    column = [tq[0, p] for p in wanted]

    def ranks(p, carry):
        return tuple(
            n + ((tq[0, p] == q) & (p < own)).astype(jnp.int32) for n, q, own in zip(carry, column, wanted)
        )

    ranked = lax.fori_loop(0, pairs, ranks, (zero,) * len(wanted))
    for i in range(4 * nx):
        loc_t[i] = lax.div(column[i], nx)
        loc_t[4 * nx + i] = jnp.minimum(ranked[i], MOST - 1)
        loc_t[8 * nx + i] = lax.rem(column[i], nx)

    for i in [0] + near:
        pass_on(1, i)
    all_arrived(0)

    for i, k in enumerate(first + second):
        g[row, i] = call[lax.div(k, nx), lax.rem(k, nx)]

    def g_has(d, t, h):
        return t < top or (h < CHUNKS // 2) == (d > 0)

    def g_ref(k, h):
        return g.at[zrel(k) * 2 + c, pl.ds(h * (2 * MOST // CHUNKS), 2 * MOST // CHUNKS)]

    def gsend(d, t, h):
        ref = g_ref(-d * (t - 1), h)
        s_sem, r_sem = (gs_p, gr_p) if d > 0 else (gs_m, gr_m)
        return pltpu.make_async_remote_copy(
            src_ref=ref, dst_ref=ref, send_sem=s_sem.at[t - 1, h], recv_sem=r_sem.at[t - 1, h],
            device_id=(y, x, zrel(d), c), device_id_type=MESH,
        )

    def grecv(d, t, h):
        ref = g_ref(-d * t, h)
        pltpu.make_async_copy(ref, ref, (gr_p if d > 0 else gr_m).at[t - 1, h]).wait()

    def sibling(zz, core, h):
        ref = g.at[zz * 2 + core, pl.ds(h * MOST, MOST)]
        return pltpu.make_async_remote_copy(
            src_ref=ref, dst_ref=ref, send_sem=ss_s.at[zz, h], recv_sem=ss_r.at[zz, h],
            device_id=(y, x, z, 1 - c), device_id_type=MESH,
        )

    def block_in(zz):
        for h in range(2):
            sibling(zz, 1 - c, h).wait_recv()

    def block_half(zz, a):
        @pl.loop(0, HALF)
        def _(i):
            s = a * HALF + i
            for core in range(2):
                for h in range(2):
                    lane = (core * 2 + h) * 128
                    one = g[zz * 2 + core, s, h * BP:(h + 1) * BP, :]
                    two = g[zz * 2 + core, MOST + s, h * BP:(h + 1) * BP, :]
                    for k in range(NB):
                        prod[i, k * BP:(k + 1) * BP, lane:lane + 128] = one[k:k + 1, :] * two
        part = pl.ds(a * HALF, HALF)
        some = jnp.dot(prod[...].reshape(HALF * NB * BP, 512), wt[zz], preferred_element_type=F32)
        acc[part] += some.reshape(HALF, NB * BP, 256)

    for h in range(CHUNKS):
        for d in (1, -1):
            if g_has(d, 1, h):
                gsend(d, 1, h).start()
    for h in range(2):
        sibling(z, c, h).start()
    before = [z]
    for t in range(1, top + 1):
        for h in range(CHUNKS):
            for d in (1, -1):
                if g_has(d, t, h):
                    grecv(d, t, h)
                    if t < top and g_has(d, t + 1, h):
                        gsend(d, t + 1, h).start()
            if (h + 1) % (CHUNKS // 2) == 0:
                half = (h + 1) // (CHUNKS // 2) - 1
                for d in (1, -1):
                    if g_has(d, t, h):
                        sibling(zrel(-d * t), c, half).start()
            piece = h * 4 // CHUNKS
            if h % (CHUNKS // 4) == 0 and piece // 2 < len(before):
                if piece % 2 == 0:
                    block_in(before[piece // 2])
                block_half(before[piece // 2], piece % 2)
        before = [zrel(-t), zrel(t)] if t < top else [zrel(t)]
    all_arrived(1)

    def pair_copy(s):
        return pltpu.make_async_remote_copy(
            src_ref=pp.at[s, 1 - c], dst_ref=rr.at[s], send_sem=p_s.at[s], recv_sem=p_r.at[s],
            device_id=(y, x, z, 1 - c), device_id_type=MESH,
        )

    def partial(s):
        one = vall[lax.div(first[s], nx), lax.rem(first[s], nx)]
        two = vall[lax.div(second[s], nx), lax.rem(second[s], nx)]
        for h in range(2):
            a, b = one[h * BP:(h + 1) * BP, :], two[h * BP:(h + 1) * BP, :]
            for k in range(NB):
                valp[k * BP:(k + 1) * BP, h * 128:(h + 1) * 128] = a[k:k + 1, :] * b
        for q in range(CG):
            it = jnp.concatenate(
                [acc[s, (q * CW + k) * BP:(q * CW + k) * BP + NB, :] for k in range(CW)]
                + [jnp.zeros((128 - CW * NB, 256), F32)], axis=0,
            ).astype(BF)
            part = lax.dot_general(valp[...], it, (((1,), (1,)), ((), ())), preferred_element_type=F32)
            for v in range(NB):
                u = v * CG + q
                r, i = u // units, u % units
                piece = part[v * BP:(v + 1) * BP, :]
                if i < CG:
                    pf[r, i * NB:(i + 1) * NB, :WIDE] = piece[:NB, :WIDE]
                else:
                    for k in range(CG):
                        moved = pltpu.roll(piece, WIDE - k * TAIL, 1)
                        pf[r, k * NB:(k + 1) * NB, WIDE:WIDE + TAIL] = moved[:NB, WIDE:WIDE + TAIL]
        for r in range(rows):
            pp[s, r % 2, r // 2] = pf[r].astype(BF)
        pair_copy(s).start()

    def qsend(d, t, s):
        out, into, s_sem, r_sem = (sp, rp, qs_p, qr_p) if d > 0 else (sm, rm, qs_m, qr_m)
        return pltpu.make_async_remote_copy(
            src_ref=out.at[t - 1, s], dst_ref=into.at[t - 1, s],
            send_sem=s_sem.at[t - 1, s], recv_sem=r_sem.at[t - 1, s],
            device_id=(y, x, zrel(d), c), device_id_type=MESH,
        )

    def first_half(d):
        return (0, HALF) if d > 0 else (HALF, MOST)

    def has(d, t, s):
        return t > 1 or first_half(d)[0] <= s < first_half(d)[1]

    def qstep(d, t, s, add):
        out, into = (sp, rp) if d > 0 else (sm, rm)
        own = pp[s, c, zrel(d * (top + 1 - t))]
        if add:
            qsend(d, t - 1, s).wait_recv()
            own = (own.astype(F32) + into[t - 2, s].astype(F32)).astype(BF)
        out[t - 1, s] = own
        qsend(d, t, s).start()

    def added(s):
        pair_copy(s).wait_recv()

        @pl.loop(0, nz)
        def _(zz):
            pp[s, c, zz] = (pp[s, c, zz].astype(F32) + rr[s, zz].astype(F32)).astype(BF)

        for d in (1, -1):
            if has(d, 1, s):
                qstep(d, 1, s, False)
            elif top > 1:
                qstep(d, 2, s, False)

    def ysend(d, t, s):
        blk = yb.at[yrel(-d * (t - 1)), s]
        s_sem, r_sem = (ys_p, yr_p) if d > 0 else (ys_m, yr_m)
        return pltpu.make_async_remote_copy(
            src_ref=blk, dst_ref=blk, send_sem=s_sem.at[t - 1, s], recv_sem=r_sem.at[t - 1, s],
            device_id=(yrel(d), x, z, c), device_id_type=MESH,
        )

    def yhas(d, t, s):
        return t < ytop or first_half(d)[0] <= s < first_half(d)[1]

    def yrecv(d, t, s):
        blk = yb.at[yrel(-d * t), s]
        pltpu.make_async_copy(blk, blk, (yr_p if d > 0 else yr_m).at[t - 1, s]).wait()

    def done(s):
        total = pp[s, c, z].astype(F32)
        for d, into in ((1, rp), (-1, rm)):
            if has(d, top, s):
                qsend(d, top, s).wait_recv()
                total = total + into[top - 1, s].astype(F32)
        yb[y, s] = total.astype(BF)
        for d in (1, -1):
            if yhas(d, 1, s):
                ysend(d, 1, s).start()

    def ystep(t, s):
        for d in (1, -1):
            if yhas(d, t, s):
                yrecv(d, t, s)
                if t < ytop and yhas(d, t + 1, s):
                    ysend(d, t + 1, s).start()

    for s in range(MOST + 1):
        if s == 0:
            for zz in before:
                block_in(zz)
        if s < MOST:
            if s % HALF == 0:
                for zz in before:
                    block_half(zz, s // HALF)
            partial(s)
        if s:
            added(s - 1)
    for t in range(2, top + 1):
        for s in range(MOST):
            for d in (1, -1):
                if t > 2 or has(d, 1, s):
                    qstep(d, t, s, True)
    for s in range(MOST):
        done(s)
    for t in range(1, ytop + 1):
        for s in range(MOST):
            ystep(t, s)

    def xcopy(i, m):
        to = xrel(i)
        part = pl.ds(m * PAIR_DEV, PAIR_DEV)
        return pltpu.make_async_remote_copy(
            src_ref=xs.at[to, part], dst_ref=(xr_d, xr_m)[m].at[x], send_sem=xs_s.at[m, i], recv_sem=xs_r.at[m, i],
            device_id=(y, to, z, c), device_id_type=MESH,
        )

    for m in (1, 0):
        for i in list(range(1, nx)) + [0]:
            to = xrel(i)
            for j in range(m * PAIR_DEV, (m + 1) * PAIR_DEV):
                got = yb[loc_t[to * 4 + j], loc_t[4 * nx + to * 4 + j]]
                if i:
                    xs[to, j] = got
                else:
                    (xr_d, xr_m)[m][to, j - m * PAIR_DEV] = got
            if i:
                xcopy(i, m).start()

    for f in fetch[3:]:
        f.wait()
    for i in range(1, nx):
        xcopy(i, 1).wait_recv()

    srows = mask_d.shape[0]
    at_r = lax.broadcasted_iota(jnp.int32, (srows, 128), 0)
    at_l = lax.broadcasted_iota(jnp.int32, (srows, 128), 1)

    def ordered(m, j, spread, mask):
        base = (xr_d, xr_m)[m][loc_t[8 * nx + x * 4 + m * PAIR_DEV + j], j].astype(F32)
        last = jnp.zeros((NB, 128), F32)
        lane = lax.broadcasted_iota(jnp.int32, (NB, 128), 1)
        for k in range(CG):
            moved = pltpu.roll(base[k * NB:(k + 1) * NB, :], 128 - (WIDE - k * TAIL), 1)
            last = jnp.where((lane >= k * TAIL) & (lane < (k + 1) * TAIL), moved, last)
        got = jnp.concatenate([base, last, jnp.zeros((srows - units * NB, 128), F32)], axis=0)
        kept = [
            jnp.where((at_r < units * NB) & (at_l >= k * NB) & (at_l < (k + 1) * NB), got, 0.0).astype(BF)
            for k in range(CW)
        ]
        parts = []
        for k in range(CW):
            wide = jnp.dot(kept[k], spread[...], preferred_element_type=F32)
            parts.append((wide * mask[...].astype(F32)).astype(BF))
        return jnp.dot(collect[...], jnp.concatenate(parts, axis=0), preferred_element_type=F32)

    rpad = up(share, 32)
    turned = jnp.concatenate(
        [ordered(1, j, spread_m, mask_m) for j in range(PAIR_DEV)]
        + [jnp.zeros((128 - PAIR_DEV * rpad, rows * rpad), F32)], axis=0,
    ).T.astype(BF)
    for r in range(rows):
        ms[r] = turned[r * rpad:(r + 1) * rpad, :]
    mr[row] = ms[row]

    def mcopy(i):
        to = lax.rem(row + i, rows)
        return pltpu.make_async_remote_copy(
            src_ref=ms.at[to], dst_ref=mr.at[row], send_sem=ms_s.at[i], recv_sem=ms_r.at[i],
            device_id=at_row(to), device_id_type=MESH,
        )

    @pl.loop(1, rows)
    def _(i):
        mcopy(i).start()

    for i in range(1, nx):
        xcopy(i, 0).wait_recv()
    out_d[...] = jnp.stack(
        [ordered(0, j, spread_d, mask_d)[:share, :NB * NB] for j in range(PAIR_DEV)], axis=1
    ).astype(BF)

    @pl.loop(1, rows)
    def _(i):
        mcopy(i).wait_recv()

    out_m[...] = jnp.stack([
        jnp.concatenate(
            [mr[r].astype(F32)[:share, j * rpad:j * rpad + share] for r in range(rows)], axis=1
        ) for j in range(PAIR_DEV)
    ], axis=1).astype(BF)

    for n in range(2):
        for i in range(ny):
            if i:
                by(n, i).wait_send()
            for k in range(1, nx):
                bx(n, i, k).wait_send()
    for t in range(1, top + 1):
        for h in range(CHUNKS):
            for d in (1, -1):
                if g_has(d, t, h):
                    gsend(d, t, h).wait_send()
    for k in range(nz):
        for h in range(2):
            sibling(k, c, h).wait_send()
    for s in range(MOST):
        pair_copy(s).wait_send()
        for t in range(1, top + 1):
            for d in (1, -1):
                if has(d, t, s):
                    qsend(d, t, s).wait_send()
        for t in range(1, ytop + 1):
            for d in (1, -1):
                if yhas(d, t, s):
                    ysend(d, t, s).wait_send()
    for m in range(2):
        for i in range(1, nx):
            xcopy(i, m).wait_send()

    @pl.loop(1, rows)
    def _(i):
        mcopy(i).wait_send()


def constants(rows):
    share = NB * NB // rows
    units = NB * CG // rows
    srows = up(units * NB, 16)
    rpad = up(share, 32)
    lane = np.arange(128)
    plain = np.arange(up(NB * NB, 128))
    wd = np.where(plain < NB * NB, plain, -1)
    padded = np.arange(rows * rpad)
    wdm = np.where(padded % rpad < share, padded // rpad * share + padded % rpad, -1)
    r = np.arange(srows)

    def two(cols):
        spread = (lane[:, None] < CW * NB) & (cols[None, :] >= 0) & (lane[:, None] % NB == cols[None, :] % NB)
        mask = (r[:, None] < units * NB) & (cols[None, :] >= 0) & (r[:, None] % NB == cols[None, :] // NB)
        return spread, mask

    k = np.arange(CW * srows)
    out = np.arange(rpad)
    rr = k % srows
    collect = (
        (rr[None, :] < units * NB) & (out[:, None] < share)
        & (rr[None, :] // NB == out[:, None] // CW) & (k[None, :] // srows == out[:, None] % CW)
    )
    return [a.astype(np.float32).astype(BF) for a in (*two(wd), *two(wdm), collect)]


def solution(mesh):
    sizes = tuple(int(np.prod([mesh.shape[a]])) for a in ("pb", "row"))
    nx, ny, nz = GRID.get(sizes, (4, 8, 8))
    split = Mesh(mesh.devices.reshape(ny, nx, nz, 2), ("y", "x", "z", "c"))
    npb, rows = ny * nx, 2 * nz
    share, units = NB * NB // rows, NB * CG // rows
    srows, rpad = up(units * NB, 16), up(share, 32)
    top, ytop = nz // 2, ny // 2
    dma = pltpu.SemaphoreType.DMA

    def shards(val, con, screened, pair_list, transfer_index, owner_map):
        pairs = pair_list.shape[0]
        consts = [jnp.asarray(a) for a in constants(rows)]
        vmem, anywhere = pl.BlockSpec(memory_space=pltpu.VMEM), pl.BlockSpec(memory_space=pl.ANY)
        points = screened.shape[2]
        blk = ((units - 1) * NB, 128)
        scratch = [
            pltpu.VMEM(val.shape, BF), pltpu.VMEM(con.shape, BF),
            pltpu.VMEM((256, points), BF),
            *[pltpu.VMEM(a.shape, BF) for a in consts],
            pltpu.VMEM((nz, 512, 256), BF),
            pltpu.VMEM((ny, nx, KB, 128), BF),
            pltpu.VMEM((ny, nx, KB, 128), BF),
            pltpu.VMEM((rows, 2 * MOST, KB, 128), BF),
            pltpu.VMEM((MOST, NB * BP, 256), F32),
            pltpu.VMEM((HALF, NB * BP, 512), BF),
            pltpu.VMEM((NB * BP, 256), BF),
            pltpu.VMEM((rows, *blk), F32),
            pltpu.VMEM((MOST, 2, nz, *blk), BF),
            pltpu.VMEM((MOST, nz, *blk), BF),
            *[pltpu.VMEM((top, MOST, *blk), BF) for _ in range(4)],
            pltpu.VMEM((ny, MOST, *blk), BF),
            pltpu.VMEM((nx, 2 * PAIR_DEV, *blk), BF),
            pltpu.VMEM((nx, PAIR_DEV, *blk), BF),
            pltpu.VMEM((nx, PAIR_DEV, *blk), BF),
            pltpu.VMEM((rows, rpad, 128), BF),
            pltpu.VMEM((rows, rpad, 128), BF),
            pltpu.SMEM((12 * nx,), jnp.int32),
            dma((8,)),
            dma((2, ny)), dma((2, ny)), dma((2, ny, nx)), dma((2, ny, nx)),
            *[dma((top, CHUNKS)) for _ in range(4)],
            dma((nz, 2)), dma((nz, 2)),
            dma((MOST,)), dma((MOST,)),
            *[dma((top, MOST)) for _ in range(4)],
            *[dma((ytop, MOST)) for _ in range(4)],
            dma((2, nx)), dma((2, nx)), dma((rows,)), dma((rows,)),
        ]
        result = jax.ShapeDtypeStruct((share, PAIR_DEV, NB * NB), BF)
        direct, mirror = pl.pallas_call(
            functools.partial(kernel, ny, nx, nz, pairs),
            out_shape=(result, result),
            in_specs=[*[pl.BlockSpec(memory_space=pltpu.SMEM)] * 3, *[anywhere] * 8],
            out_specs=(vmem, vmem),
            scratch_shapes=scratch,
            compiler_params=pltpu.CompilerParams(
                collective_id=0, has_side_effects=True, vmem_limit_bytes=60 * 2**20
            ),
        )(transfer_index.T, pair_list.T, owner_map, val, con, screened, *consts)
        return direct.transpose(1, 0, 2), mirror.transpose(1, 0, 2)

    in_specs = (P(("y", "x"), None, ("z", "c")), P(("y", "x"), None, ("z", "c")),
                P(("y", "x"), ("z", "c"), None), P(), P(), P())
    out = P(("y", "x"), ("z", "c"), None)
    return jax.shard_map(shards, mesh=split, in_specs=in_specs, out_specs=(out, out), check_vma=False)


GRID = {(4, 4): (2, 2, 2), (2, 8): (1, 2, 4)}
```

```python
import functools

import jax
import jax.numpy as jnp
import numpy as np
from jax import lax
from jax.experimental import pallas as pl
from jax.experimental.pallas import tpu as pltpu
from jax.sharding import Mesh
from jax.sharding import PartitionSpec as P

MESH = pl.DeviceIdType.MESH
BF = jnp.bfloat16
F32 = jnp.float32
NB = 20
BP = 24
KB = 2 * BP
CG = 4
CW = NB // CG
WIDE = CW * NB
TAIL = WIDE // CG
PAIR_DEV = 2
MOST = 6
HALF = MOST // 2
CHUNKS = 4


def up(n, to):
    return -(-n // to) * to


def kernel(
    ny, nx, nz, pairs,
    tq, tp, to_slot, val_any, con_any, w_any, spread_d_any, mask_d_any, spread_m_any, mask_m_any, collect_any,
    out_d, out_m,
    val, con, w, spread_d, mask_d, spread_m, mask_m, collect,
    wt, call, vall, g, acc, prod, valp, pf, pp, rr, rp, rm, sp, sm, yb, xs, xr_d, xr_m, ms, mr,
    loc_t, loc,
    by_s, by_r, bx_s, bx_r,
    gs_p, gr_p, gs_m, gr_m, ss_s, ss_r,
    p_s, p_r, qs_p, qr_p, qs_m, qr_m,
    ys_p, yr_p, ys_m, yr_m, xs_s, xs_r, ms_s, ms_r,
):
    y, x, z, c = (lax.axis_index(a) for a in ("y", "x", "z", "c"))
    rows = 2 * nz
    me = y * nx + x
    row = z * 2 + c
    share = NB * NB // rows
    units = NB * CG // rows
    top, ytop = nz // 2, ny // 2

    def at_row(r):
        return (y, x, r // 2, lax.rem(r, 2))

    def zrel(k):
        return lax.rem(z + k + 2 * nz, nz)

    def yrel(k):
        return lax.rem(y + k + 2 * ny, ny)

    def xrel(k):
        return lax.rem(x + k + 2 * nx, nx)

    barrier = pltpu.get_barrier_semaphore()
    for i in range(1, nx):
        pl.semaphore_signal(barrier, inc=1, device_id=(y, xrel(i), z, c), device_id_type=MESH)
    for i in range(1, ny):
        pl.semaphore_signal(barrier, inc=1, device_id=(yrel(i), x, z, c), device_id_type=MESH)

    @pl.loop(1, rows)
    def _(i):
        pl.semaphore_signal(barrier, inc=1, device_id=at_row(lax.rem(row + i, rows)), device_id_type=MESH)

    fetch = [
        pltpu.make_async_copy(a, b, loc.at[i])
        for i, (a, b) in enumerate((
            (con_any, con), (val_any, val), (w_any.at[0], w), (spread_d_any, spread_d), (mask_d_any, mask_d),
            (spread_m_any, spread_m), (mask_m_any, mask_m), (collect_any, collect),
        ))
    ]
    for f in fetch:
        f.start()

    def stage(buf, src):
        blank = jnp.zeros((BP - NB, 128), BF)
        for h in range(2):
            part = src[0, :, h * 128:(h + 1) * 128]
            buf[y, x, h * BP:(h + 1) * BP, :] = jnp.concatenate([part, blank], axis=0)

    fetch[0].wait()
    stage(call, con)
    fetch[1].wait()
    stage(vall, val)
    pl.semaphore_wait(barrier, nx - 1 + ny - 1 + rows - 1)

    near = sorted(range(1, ny), key=lambda i: min(i, ny - i))

    def by(n, i):
        ref = (call, vall)[n].at[y, x]
        return pltpu.make_async_remote_copy(
            src_ref=ref, dst_ref=ref, send_sem=by_s.at[n, i], recv_sem=by_r.at[n, i],
            device_id=(yrel(i), x, z, c), device_id_type=MESH,
        )

    def bx(n, i, k):
        ref = (call, vall)[n].at[yrel(-i), x]
        return pltpu.make_async_remote_copy(
            src_ref=ref, dst_ref=ref, send_sem=bx_s.at[n, i, k], recv_sem=bx_r.at[n, i, k],
            device_id=(y, xrel(k), z, c), device_id_type=MESH,
        )

    def b_arrived(n, i, k):
        ref = (call, vall)[n].at[yrel(-i), xrel(-k)]
        pltpu.make_async_copy(ref, ref, bx_r.at[n, i, k] if k else by_r.at[n, i]).wait()

    def pass_on(n, i):
        if i:
            b_arrived(n, i, 0)
        for k in range(1, nx):
            bx(n, i, k).start()

    def all_arrived(n):
        for i in [0] + near:
            for k in range(1, nx):
                b_arrived(n, i, k)

    pass_on(0, 0)
    for n in range(2):
        for i in near:
            by(n, i).start()

    pf[...] = jnp.zeros(pf.shape, F32)

    @pl.loop(0, MOST)
    def _(s):
        acc[s] = jnp.zeros(acc.shape[1:], F32)

    for i in near:
        pass_on(0, i)

    fetch[2].wait()
    for zz in range(nz):
        wt[zz] = w[:, zz * 512:(zz + 1) * 512].T

    def owner(k):
        return to_slot[k]

    def own_slots(p, carry):
        count, slots = carry
        hit = tq[0, p] == me
        slots = tuple(jnp.where(hit & (count == s), p, slots[s]) for s in range(MOST))
        return count + hit.astype(jnp.int32), slots

    zero = jnp.int32(0)
    _, slots = lax.fori_loop(0, pairs, own_slots, (zero, (zero,) * MOST))
    first = [owner(tp[0, p]) for p in slots]
    second = [owner(tp[1, p]) for p in slots]

    def by_second(p, carry):
        e = owner(tp[1, p])
        new = []
        for k in range(nx):
            count, one, two = carry[k]
            hit = e == y * nx + k
            new.append((count + hit.astype(jnp.int32), jnp.where(hit & (count == 0), p, one),
                        jnp.where(hit & (count == 1), p, two)))
        return tuple(new)

    found = lax.fori_loop(0, pairs, by_second, ((zero,) * 3,) * nx)
    wanted = []
    for k in range(nx):
        at = (y * nx + k) * PAIR_DEV
        wanted += [at, at + 1, found[k][1], found[k][2]]
    column = [tq[0, p] for p in wanted]

    def ranks(p, carry):
        return tuple(
            n + ((tq[0, p] == q) & (p < own)).astype(jnp.int32) for n, q, own in zip(carry, column, wanted)
        )

    ranked = lax.fori_loop(0, pairs, ranks, (zero,) * len(wanted))
    for i in range(4 * nx):
        loc_t[i] = lax.div(column[i], nx)
        loc_t[4 * nx + i] = jnp.minimum(ranked[i], MOST - 1)
        loc_t[8 * nx + i] = lax.rem(column[i], nx)

    for i in [0] + near:
        pass_on(1, i)
    all_arrived(0)

    for i, k in enumerate(first + second):
        g[row, i] = call[lax.div(k, nx), lax.rem(k, nx)]

    def g_has(d, t, h):
        return t < top or (h < CHUNKS // 2) == (d > 0)

    def g_ref(k, h):
        return g.at[zrel(k) * 2 + c, pl.ds(h * (2 * MOST // CHUNKS), 2 * MOST // CHUNKS)]

    def gsend(d, t, h):
        ref = g_ref(-d * (t - 1), h)
        s_sem, r_sem = (gs_p, gr_p) if d > 0 else (gs_m, gr_m)
        return pltpu.make_async_remote_copy(
            src_ref=ref, dst_ref=ref, send_sem=s_sem.at[t - 1, h], recv_sem=r_sem.at[t - 1, h],
            device_id=(y, x, zrel(d), c), device_id_type=MESH,
        )

    def grecv(d, t, h):
        ref = g_ref(-d * t, h)
        pltpu.make_async_copy(ref, ref, (gr_p if d > 0 else gr_m).at[t - 1, h]).wait()

    def sibling(zz, core, h):
        ref = g.at[zz * 2 + core, pl.ds(h * MOST, MOST)]
        return pltpu.make_async_remote_copy(
            src_ref=ref, dst_ref=ref, send_sem=ss_s.at[zz, h], recv_sem=ss_r.at[zz, h],
            device_id=(y, x, z, 1 - c), device_id_type=MESH,
        )

    def block_slot(zz, s):
        for core in range(2):
            for h in range(2):
                lane = (core * 2 + h) * 128
                one = g[zz * 2 + core, s, h * BP:(h + 1) * BP, :]
                two = g[zz * 2 + core, MOST + s, h * BP:(h + 1) * BP, :]
                for k in range(NB):
                    prod[k * BP:(k + 1) * BP, lane:lane + 128] = one[k:k + 1, :] * two
        acc[s] += jnp.dot(prod[...], wt[zz], preferred_element_type=F32)

    def block_in(zz):
        for h in range(2):
            sibling(zz, 1 - c, h).wait_recv()

    def block(zz):
        block_in(zz)

        @pl.loop(0, MOST)
        def _(s):
            block_slot(zz, s)

    for h in range(CHUNKS):
        for d in (1, -1):
            if g_has(d, 1, h):
                gsend(d, 1, h).start()
    for h in range(2):
        sibling(z, c, h).start()
    before = [z]
    for t in range(1, top + 1):
        for h in range(CHUNKS):
            for d in (1, -1):
                if g_has(d, t, h):
                    grecv(d, t, h)
                    if t < top and g_has(d, t + 1, h):
                        gsend(d, t + 1, h).start()
            if (h + 1) % (CHUNKS // 2) == 0:
                half = (h + 1) // (CHUNKS // 2) - 1
                for d in (1, -1):
                    if g_has(d, t, h):
                        sibling(zrel(-d * t), c, half).start()
                if half < len(before):
                    block(before[half])
        before = [zrel(-t), zrel(t)] if t < top else [zrel(t)]
    all_arrived(1)

    def pair_copy(s):
        return pltpu.make_async_remote_copy(
            src_ref=pp.at[s, 1 - c], dst_ref=rr.at[s], send_sem=p_s.at[s], recv_sem=p_r.at[s],
            device_id=(y, x, z, 1 - c), device_id_type=MESH,
        )

    def partial(s):
        one = vall[lax.div(first[s], nx), lax.rem(first[s], nx)]
        two = vall[lax.div(second[s], nx), lax.rem(second[s], nx)]
        for h in range(2):
            a, b = one[h * BP:(h + 1) * BP, :], two[h * BP:(h + 1) * BP, :]
            for k in range(NB):
                valp[k * BP:(k + 1) * BP, h * 128:(h + 1) * 128] = a[k:k + 1, :] * b
        for q in range(CG):
            it = jnp.concatenate(
                [acc[s, (q * CW + k) * BP:(q * CW + k) * BP + NB, :] for k in range(CW)]
                + [jnp.zeros((128 - CW * NB, 256), F32)], axis=0,
            ).astype(BF)
            part = lax.dot_general(valp[...], it, (((1,), (1,)), ((), ())), preferred_element_type=F32)
            for v in range(NB):
                u = v * CG + q
                r, i = u // units, u % units
                piece = part[v * BP:(v + 1) * BP, :]
                if i < CG:
                    pf[r, i * NB:(i + 1) * NB, :WIDE] = piece[:NB, :WIDE]
                else:
                    for k in range(CG):
                        moved = pltpu.roll(piece, WIDE - k * TAIL, 1)
                        pf[r, k * NB:(k + 1) * NB, WIDE:WIDE + TAIL] = moved[:NB, WIDE:WIDE + TAIL]
        for r in range(rows):
            pp[s, r % 2, r // 2] = pf[r].astype(BF)
        pair_copy(s).start()

    def qsend(d, t, s):
        out, into, s_sem, r_sem = (sp, rp, qs_p, qr_p) if d > 0 else (sm, rm, qs_m, qr_m)
        return pltpu.make_async_remote_copy(
            src_ref=out.at[t - 1, s], dst_ref=into.at[t - 1, s],
            send_sem=s_sem.at[t - 1, s], recv_sem=r_sem.at[t - 1, s],
            device_id=(y, x, zrel(d), c), device_id_type=MESH,
        )

    def first_half(d):
        return (0, HALF) if d > 0 else (HALF, MOST)

    def has(d, t, s):
        return t > 1 or first_half(d)[0] <= s < first_half(d)[1]

    def qstep(d, t, s, add):
        out, into = (sp, rp) if d > 0 else (sm, rm)
        own = pp[s, c, zrel(d * (top + 1 - t))]
        if add:
            qsend(d, t - 1, s).wait_recv()
            own = (own.astype(F32) + into[t - 2, s].astype(F32)).astype(BF)
        out[t - 1, s] = own
        qsend(d, t, s).start()

    def added(s):
        pair_copy(s).wait_recv()

        @pl.loop(0, nz)
        def _(zz):
            pp[s, c, zz] = (pp[s, c, zz].astype(F32) + rr[s, zz].astype(F32)).astype(BF)

        for d in (1, -1):
            if has(d, 1, s):
                qstep(d, 1, s, False)
            elif top > 1:
                qstep(d, 2, s, False)

    def ysend(d, t, s):
        blk = yb.at[yrel(-d * (t - 1)), s]
        s_sem, r_sem = (ys_p, yr_p) if d > 0 else (ys_m, yr_m)
        return pltpu.make_async_remote_copy(
            src_ref=blk, dst_ref=blk, send_sem=s_sem.at[t - 1, s], recv_sem=r_sem.at[t - 1, s],
            device_id=(yrel(d), x, z, c), device_id_type=MESH,
        )

    def yhas(d, t, s):
        return t < ytop or first_half(d)[0] <= s < first_half(d)[1]

    def yrecv(d, t, s):
        blk = yb.at[yrel(-d * t), s]
        pltpu.make_async_copy(blk, blk, (yr_p if d > 0 else yr_m).at[t - 1, s]).wait()

    def done(s):
        total = pp[s, c, z].astype(F32)
        for d, into in ((1, rp), (-1, rm)):
            if has(d, top, s):
                qsend(d, top, s).wait_recv()
                total = total + into[top - 1, s].astype(F32)
        yb[y, s] = total.astype(BF)
        for d in (1, -1):
            if yhas(d, 1, s):
                ysend(d, 1, s).start()

    def ystep(t, s):
        for d in (1, -1):
            if yhas(d, t, s):
                yrecv(d, t, s)
                if t < ytop and yhas(d, t + 1, s):
                    ysend(d, t + 1, s).start()

    for s in range(MOST + 1):
        if s == 0:
            for zz in before:
                block_in(zz)
        if s < MOST:
            for zz in before:
                block_slot(zz, s)
            partial(s)
        if s:
            added(s - 1)
    for t in range(2, top + 1):
        for s in range(MOST):
            for d in (1, -1):
                if t > 2 or has(d, 1, s):
                    qstep(d, t, s, True)
    for s in range(MOST):
        done(s)
    for t in range(1, ytop + 1):
        for s in range(MOST):
            ystep(t, s)

    def xcopy(i, m):
        to = xrel(i)
        part = pl.ds(m * PAIR_DEV, PAIR_DEV)
        return pltpu.make_async_remote_copy(
            src_ref=xs.at[to, part], dst_ref=(xr_d, xr_m)[m].at[x], send_sem=xs_s.at[m, i], recv_sem=xs_r.at[m, i],
            device_id=(y, to, z, c), device_id_type=MESH,
        )

    for m in (1, 0):
        for i in list(range(1, nx)) + [0]:
            to = xrel(i)
            for j in range(m * PAIR_DEV, (m + 1) * PAIR_DEV):
                got = yb[loc_t[to * 4 + j], loc_t[4 * nx + to * 4 + j]]
                if i:
                    xs[to, j] = got
                else:
                    (xr_d, xr_m)[m][to, j - m * PAIR_DEV] = got
            if i:
                xcopy(i, m).start()

    for f in fetch[3:]:
        f.wait()
    for i in range(1, nx):
        xcopy(i, 1).wait_recv()

    srows = mask_d.shape[0]
    at_r = lax.broadcasted_iota(jnp.int32, (srows, 128), 0)
    at_l = lax.broadcasted_iota(jnp.int32, (srows, 128), 1)

    def ordered(m, j, spread, mask):
        base = (xr_d, xr_m)[m][loc_t[8 * nx + x * 4 + m * PAIR_DEV + j], j].astype(F32)
        last = jnp.zeros((NB, 128), F32)
        lane = lax.broadcasted_iota(jnp.int32, (NB, 128), 1)
        for k in range(CG):
            moved = pltpu.roll(base[k * NB:(k + 1) * NB, :], 128 - (WIDE - k * TAIL), 1)
            last = jnp.where((lane >= k * TAIL) & (lane < (k + 1) * TAIL), moved, last)
        got = jnp.concatenate([base, last, jnp.zeros((srows - units * NB, 128), F32)], axis=0)
        kept = [
            jnp.where((at_r < units * NB) & (at_l >= k * NB) & (at_l < (k + 1) * NB), got, 0.0).astype(BF)
            for k in range(CW)
        ]
        parts = []
        for k in range(CW):
            wide = jnp.dot(kept[k], spread[...], preferred_element_type=F32)
            parts.append((wide * mask[...].astype(F32)).astype(BF))
        return jnp.dot(collect[...], jnp.concatenate(parts, axis=0), preferred_element_type=F32)

    rpad = up(share, 32)
    turned = jnp.concatenate(
        [ordered(1, j, spread_m, mask_m) for j in range(PAIR_DEV)]
        + [jnp.zeros((128 - PAIR_DEV * rpad, rows * rpad), F32)], axis=0,
    ).T.astype(BF)
    for r in range(rows):
        ms[r] = turned[r * rpad:(r + 1) * rpad, :]
    mr[row] = ms[row]

    def mcopy(i):
        to = lax.rem(row + i, rows)
        return pltpu.make_async_remote_copy(
            src_ref=ms.at[to], dst_ref=mr.at[row], send_sem=ms_s.at[i], recv_sem=ms_r.at[i],
            device_id=at_row(to), device_id_type=MESH,
        )

    @pl.loop(1, rows)
    def _(i):
        mcopy(i).start()

    for i in range(1, nx):
        xcopy(i, 0).wait_recv()
    out_d[...] = jnp.stack(
        [ordered(0, j, spread_d, mask_d)[:share, :NB * NB] for j in range(PAIR_DEV)], axis=1
    ).astype(BF)

    @pl.loop(1, rows)
    def _(i):
        mcopy(i).wait_recv()

    out_m[...] = jnp.stack([
        jnp.concatenate(
            [mr[r].astype(F32)[:share, j * rpad:j * rpad + share] for r in range(rows)], axis=1
        ) for j in range(PAIR_DEV)
    ], axis=1).astype(BF)

    for n in range(2):
        for i in range(ny):
            if i:
                by(n, i).wait_send()
            for k in range(1, nx):
                bx(n, i, k).wait_send()
    for t in range(1, top + 1):
        for h in range(CHUNKS):
            for d in (1, -1):
                if g_has(d, t, h):
                    gsend(d, t, h).wait_send()
    for k in range(nz):
        for h in range(2):
            sibling(k, c, h).wait_send()
    for s in range(MOST):
        pair_copy(s).wait_send()
        for t in range(1, top + 1):
            for d in (1, -1):
                if has(d, t, s):
                    qsend(d, t, s).wait_send()
        for t in range(1, ytop + 1):
            for d in (1, -1):
                if yhas(d, t, s):
                    ysend(d, t, s).wait_send()
    for m in range(2):
        for i in range(1, nx):
            xcopy(i, m).wait_send()

    @pl.loop(1, rows)
    def _(i):
        mcopy(i).wait_send()


def constants(rows):
    share = NB * NB // rows
    units = NB * CG // rows
    srows = up(units * NB, 16)
    rpad = up(share, 32)
    lane = np.arange(128)
    plain = np.arange(up(NB * NB, 128))
    wd = np.where(plain < NB * NB, plain, -1)
    padded = np.arange(rows * rpad)
    wdm = np.where(padded % rpad < share, padded // rpad * share + padded % rpad, -1)
    r = np.arange(srows)

    def two(cols):
        spread = (lane[:, None] < CW * NB) & (cols[None, :] >= 0) & (lane[:, None] % NB == cols[None, :] % NB)
        mask = (r[:, None] < units * NB) & (cols[None, :] >= 0) & (r[:, None] % NB == cols[None, :] // NB)
        return spread, mask

    k = np.arange(CW * srows)
    out = np.arange(rpad)
    rr = k % srows
    collect = (
        (rr[None, :] < units * NB) & (out[:, None] < share)
        & (rr[None, :] // NB == out[:, None] // CW) & (k[None, :] // srows == out[:, None] % CW)
    )
    return [a.astype(np.float32).astype(BF) for a in (*two(wd), *two(wdm), collect)]


def solution(mesh):
    sizes = tuple(int(np.prod([mesh.shape[a]])) for a in ("pb", "row"))
    nx, ny, nz = GRID.get(sizes, (4, 8, 8))
    split = Mesh(mesh.devices.reshape(ny, nx, nz, 2), ("y", "x", "z", "c"))
    npb, rows = ny * nx, 2 * nz
    share, units = NB * NB // rows, NB * CG // rows
    srows, rpad = up(units * NB, 16), up(share, 32)
    top, ytop = nz // 2, ny // 2
    dma = pltpu.SemaphoreType.DMA

    def shards(val, con, screened, pair_list, transfer_index, owner_map):
        pairs = pair_list.shape[0]
        consts = [jnp.asarray(a) for a in constants(rows)]
        vmem, anywhere = pl.BlockSpec(memory_space=pltpu.VMEM), pl.BlockSpec(memory_space=pl.ANY)
        points = screened.shape[2]
        blk = ((units - 1) * NB, 128)
        scratch = [
            pltpu.VMEM(val.shape, BF), pltpu.VMEM(con.shape, BF),
            pltpu.VMEM((256, points), BF),
            *[pltpu.VMEM(a.shape, BF) for a in consts],
            pltpu.VMEM((nz, 512, 256), BF),
            pltpu.VMEM((ny, nx, KB, 128), BF),
            pltpu.VMEM((ny, nx, KB, 128), BF),
            pltpu.VMEM((rows, 2 * MOST, KB, 128), BF),
            pltpu.VMEM((MOST, NB * BP, 256), F32),
            pltpu.VMEM((NB * BP, 512), BF),
            pltpu.VMEM((NB * BP, 256), BF),
            pltpu.VMEM((rows, *blk), F32),
            pltpu.VMEM((MOST, 2, nz, *blk), BF),
            pltpu.VMEM((MOST, nz, *blk), BF),
            *[pltpu.VMEM((top, MOST, *blk), BF) for _ in range(4)],
            pltpu.VMEM((ny, MOST, *blk), BF),
            pltpu.VMEM((nx, 2 * PAIR_DEV, *blk), BF),
            pltpu.VMEM((nx, PAIR_DEV, *blk), BF),
            pltpu.VMEM((nx, PAIR_DEV, *blk), BF),
            pltpu.VMEM((rows, rpad, 128), BF),
            pltpu.VMEM((rows, rpad, 128), BF),
            pltpu.SMEM((12 * nx,), jnp.int32),
            dma((8,)),
            dma((2, ny)), dma((2, ny)), dma((2, ny, nx)), dma((2, ny, nx)),
            *[dma((top, CHUNKS)) for _ in range(4)],
            dma((nz, 2)), dma((nz, 2)),
            dma((MOST,)), dma((MOST,)),
            *[dma((top, MOST)) for _ in range(4)],
            *[dma((ytop, MOST)) for _ in range(4)],
            dma((2, nx)), dma((2, nx)), dma((rows,)), dma((rows,)),
        ]
        result = jax.ShapeDtypeStruct((share, PAIR_DEV, NB * NB), BF)
        direct, mirror = pl.pallas_call(
            functools.partial(kernel, ny, nx, nz, pairs),
            out_shape=(result, result),
            in_specs=[*[pl.BlockSpec(memory_space=pltpu.SMEM)] * 3, *[anywhere] * 8],
            out_specs=(vmem, vmem),
            scratch_shapes=scratch,
            compiler_params=pltpu.CompilerParams(
                collective_id=0, has_side_effects=True, vmem_limit_bytes=60 * 2**20
            ),
        )(transfer_index.T, pair_list.T, owner_map, val, con, screened, *consts)
        return direct.transpose(1, 0, 2), mirror.transpose(1, 0, 2)

    in_specs = (P(("y", "x"), None, ("z", "c")), P(("y", "x"), None, ("z", "c")),
                P(("y", "x"), ("z", "c"), None), P(), P(), P())
    out = P(("y", "x"), ("z", "c"), None)
    return jax.shard_map(shards, mesh=split, in_specs=in_specs, out_specs=(out, out), check_vma=False)


GRID = {(4, 4): (2, 2, 2), (2, 8): (1, 2, 4)}
```

```python
import functools

import jax
import jax.numpy as jnp
import numpy as np
from jax import lax
from jax.experimental import pallas as pl
from jax.experimental.pallas import tpu as pltpu
from jax.sharding import Mesh
from jax.sharding import PartitionSpec as P

MESH = pl.DeviceIdType.MESH
BF = jnp.bfloat16
F32 = jnp.float32
NB = 20
BP = 24
KB = 2 * BP
CG = 4
CW = NB // CG
WIDE = CW * NB
TAIL = WIDE // CG
PAIR_DEV = 2
MOST = 6
HALF = MOST // 2
CHUNKS = 2


def up(n, to):
    return -(-n // to) * to


def kernel(
    ny, nx, nz, pairs,
    tq, tp, to_slot, val_any, con_any, w_any, spread_d_any, mask_d_any, spread_m_any, mask_m_any, collect_any,
    out_d, out_m,
    val, con, w, spread_d, mask_d, spread_m, mask_m, collect,
    call, vall, g, acc, prod, valp, pf, pp, rr, rp, rm, sp, sm, yb, xs, xr_d, xr_m, ms, mr,
    loc_t, loc,
    by_s, by_r, bx_s, bx_r,
    gs_p, gr_p, gs_m, gr_m, ss_s, ss_r,
    p_s, p_r, qs_p, qr_p, qs_m, qr_m,
    ys_p, yr_p, ys_m, yr_m, xs_s, xs_r, ms_s, ms_r,
):
    y, x, z, c = (lax.axis_index(a) for a in ("y", "x", "z", "c"))
    rows = 2 * nz
    me = y * nx + x
    row = z * 2 + c
    share = NB * NB // rows
    units = NB * CG // rows
    top, ytop = nz // 2, ny // 2

    def at_row(r):
        return (y, x, r // 2, lax.rem(r, 2))

    def zrel(k):
        return lax.rem(z + k + 2 * nz, nz)

    def yrel(k):
        return lax.rem(y + k + 2 * ny, ny)

    def xrel(k):
        return lax.rem(x + k + 2 * nx, nx)

    barrier = pltpu.get_barrier_semaphore()
    for i in range(1, nx):
        pl.semaphore_signal(barrier, inc=1, device_id=(y, xrel(i), z, c), device_id_type=MESH)
    for i in range(1, ny):
        pl.semaphore_signal(barrier, inc=1, device_id=(yrel(i), x, z, c), device_id_type=MESH)

    @pl.loop(1, rows)
    def _(i):
        pl.semaphore_signal(barrier, inc=1, device_id=at_row(lax.rem(row + i, rows)), device_id_type=MESH)

    fetch = [
        pltpu.make_async_copy(a, b, loc.at[i])
        for i, (a, b) in enumerate((
            (con_any, con), (val_any, val), (w_any.at[0], w), (spread_d_any, spread_d), (mask_d_any, mask_d),
            (spread_m_any, spread_m), (mask_m_any, mask_m), (collect_any, collect),
        ))
    ]
    for f in fetch:
        f.start()

    def stage(buf, src):
        blank = jnp.zeros((BP - NB, 128), BF)
        for h in range(2):
            part = src[0, :, h * 128:(h + 1) * 128]
            buf[y, x, h * BP:(h + 1) * BP, :] = jnp.concatenate([part, blank], axis=0)

    fetch[0].wait()
    stage(call, con)
    fetch[1].wait()
    stage(vall, val)
    pl.semaphore_wait(barrier, nx - 1 + ny - 1 + rows - 1)

    near = sorted(range(1, ny), key=lambda i: min(i, ny - i))

    def by(n, i):
        ref = (call, vall)[n].at[y, x]
        return pltpu.make_async_remote_copy(
            src_ref=ref, dst_ref=ref, send_sem=by_s.at[n, i], recv_sem=by_r.at[n, i],
            device_id=(yrel(i), x, z, c), device_id_type=MESH,
        )

    def bx(n, i, k):
        ref = (call, vall)[n].at[yrel(-i), x]
        return pltpu.make_async_remote_copy(
            src_ref=ref, dst_ref=ref, send_sem=bx_s.at[n, i, k], recv_sem=bx_r.at[n, i, k],
            device_id=(y, xrel(k), z, c), device_id_type=MESH,
        )

    def b_arrived(n, i, k):
        ref = (call, vall)[n].at[yrel(-i), xrel(-k)]
        pltpu.make_async_copy(ref, ref, bx_r.at[n, i, k] if k else by_r.at[n, i]).wait()

    def pass_on(n, i):
        if i:
            b_arrived(n, i, 0)
        for k in range(1, nx):
            bx(n, i, k).start()

    def all_arrived(n):
        for i in [0] + near:
            for k in range(1, nx):
                b_arrived(n, i, k)

    pass_on(0, 0)
    for n in range(2):
        for i in near:
            by(n, i).start()

    pf[...] = jnp.zeros(pf.shape, F32)

    @pl.loop(0, MOST)
    def _(s):
        acc[s] = jnp.zeros(acc.shape[1:], F32)

    for i in near:
        pass_on(0, i)

    def owner(k):
        return to_slot[k]

    def own_slots(p, carry):
        count, slots = carry
        hit = tq[0, p] == me
        slots = tuple(jnp.where(hit & (count == s), p, slots[s]) for s in range(MOST))
        return count + hit.astype(jnp.int32), slots

    zero = jnp.int32(0)
    _, slots = lax.fori_loop(0, pairs, own_slots, (zero, (zero,) * MOST))
    first = [owner(tp[0, p]) for p in slots]
    second = [owner(tp[1, p]) for p in slots]

    def by_second(p, carry):
        e = owner(tp[1, p])
        new = []
        for k in range(nx):
            count, one, two = carry[k]
            hit = e == y * nx + k
            new.append((count + hit.astype(jnp.int32), jnp.where(hit & (count == 0), p, one),
                        jnp.where(hit & (count == 1), p, two)))
        return tuple(new)

    found = lax.fori_loop(0, pairs, by_second, ((zero,) * 3,) * nx)
    wanted = []
    for k in range(nx):
        at = (y * nx + k) * PAIR_DEV
        wanted += [at, at + 1, found[k][1], found[k][2]]
    column = [tq[0, p] for p in wanted]

    def ranks(p, carry):
        return tuple(
            n + ((tq[0, p] == q) & (p < own)).astype(jnp.int32) for n, q, own in zip(carry, column, wanted)
        )

    ranked = lax.fori_loop(0, pairs, ranks, (zero,) * len(wanted))
    for i in range(4 * nx):
        loc_t[i] = lax.div(column[i], nx)
        loc_t[4 * nx + i] = jnp.minimum(ranked[i], MOST - 1)
        loc_t[8 * nx + i] = lax.rem(column[i], nx)

    for i in [0] + near:
        pass_on(1, i)
    all_arrived(0)

    for i, k in enumerate(first + second):
        g[row, i] = call[lax.div(k, nx), lax.rem(k, nx)]

    def g_has(d, t, h):
        return t < top or (h < CHUNKS // 2) == (d > 0)

    def g_ref(k, h):
        return g.at[zrel(k) * 2 + c, pl.ds(h * (2 * MOST // CHUNKS), 2 * MOST // CHUNKS)]

    def gsend(d, t, h):
        ref = g_ref(-d * (t - 1), h)
        s_sem, r_sem = (gs_p, gr_p) if d > 0 else (gs_m, gr_m)
        return pltpu.make_async_remote_copy(
            src_ref=ref, dst_ref=ref, send_sem=s_sem.at[t - 1, h], recv_sem=r_sem.at[t - 1, h],
            device_id=(y, x, zrel(d), c), device_id_type=MESH,
        )

    def grecv(d, t, h):
        ref = g_ref(-d * t, h)
        pltpu.make_async_copy(ref, ref, (gr_p if d > 0 else gr_m).at[t - 1, h]).wait()

    def sibling(zz, core, h):
        ref = g.at[zz * 2 + core, pl.ds(h * MOST, MOST)]
        return pltpu.make_async_remote_copy(
            src_ref=ref, dst_ref=ref, send_sem=ss_s.at[zz, h], recv_sem=ss_r.at[zz, h],
            device_id=(y, x, z, 1 - c), device_id_type=MESH,
        )

    def block_slot(zz, s):
        for core in range(2):
            for h in range(2):
                lane = (core * 2 + h) * 128
                one = g[zz * 2 + core, s, h * BP:(h + 1) * BP, :]
                two = g[zz * 2 + core, MOST + s, h * BP:(h + 1) * BP, :]
                for k in range(NB):
                    prod[k * BP:(k + 1) * BP, lane:lane + 128] = one[k:k + 1, :] * two
        cols = pl.ds(pl.multiple_of(zz * 512, 512), 512)
        acc[s] += lax.dot_general(
            prod[...], w[:, cols], (((1,), (1,)), ((), ())), preferred_element_type=F32
        )

    def block_in(zz):
        for h in range(2):
            sibling(zz, 1 - c, h).wait_recv()

    def block(zz):
        block_in(zz)

        @pl.loop(0, MOST)
        def _(s):
            block_slot(zz, s)

    for h in range(CHUNKS):
        for d in (1, -1):
            if g_has(d, 1, h):
                gsend(d, 1, h).start()
    for h in range(2):
        sibling(z, c, h).start()
    fetch[2].wait()
    before = [z]
    for t in range(1, top + 1):
        for h in range(CHUNKS):
            for d in (1, -1):
                if g_has(d, t, h):
                    grecv(d, t, h)
                    if t < top and g_has(d, t + 1, h):
                        gsend(d, t + 1, h).start()
            if (h + 1) % (CHUNKS // 2) == 0:
                half = (h + 1) // (CHUNKS // 2) - 1
                for d in (1, -1):
                    if g_has(d, t, h):
                        sibling(zrel(-d * t), c, half).start()
                if half < len(before):
                    block(before[half])
        before = [zrel(-t), zrel(t)] if t < top else [zrel(t)]
    all_arrived(1)

    def pair_copy(s):
        return pltpu.make_async_remote_copy(
            src_ref=pp.at[s, 1 - c], dst_ref=rr.at[s], send_sem=p_s.at[s], recv_sem=p_r.at[s],
            device_id=(y, x, z, 1 - c), device_id_type=MESH,
        )

    def partial(s):
        one = vall[lax.div(first[s], nx), lax.rem(first[s], nx)]
        two = vall[lax.div(second[s], nx), lax.rem(second[s], nx)]
        for h in range(2):
            a, b = one[h * BP:(h + 1) * BP, :], two[h * BP:(h + 1) * BP, :]
            for k in range(NB):
                valp[k * BP:(k + 1) * BP, h * 128:(h + 1) * 128] = a[k:k + 1, :] * b
        for q in range(CG):
            it = jnp.concatenate(
                [acc[s, (q * CW + k) * BP:(q * CW + k) * BP + NB, :] for k in range(CW)]
                + [jnp.zeros((128 - CW * NB, 256), F32)], axis=0,
            ).astype(BF)
            part = lax.dot_general(valp[...], it, (((1,), (1,)), ((), ())), preferred_element_type=F32)
            for v in range(NB):
                u = v * CG + q
                r, i = u // units, u % units
                piece = part[v * BP:(v + 1) * BP, :]
                if i < CG:
                    pf[r, i * NB:(i + 1) * NB, :WIDE] = piece[:NB, :WIDE]
                else:
                    for k in range(CG):
                        moved = pltpu.roll(piece, WIDE - k * TAIL, 1)
                        pf[r, k * NB:(k + 1) * NB, WIDE:WIDE + TAIL] = moved[:NB, WIDE:WIDE + TAIL]
        for r in range(rows):
            pp[s, r % 2, r // 2] = pf[r].astype(BF)
        pair_copy(s).start()

    def qsend(d, t, s):
        out, into, s_sem, r_sem = (sp, rp, qs_p, qr_p) if d > 0 else (sm, rm, qs_m, qr_m)
        return pltpu.make_async_remote_copy(
            src_ref=out.at[t - 1, s], dst_ref=into.at[t - 1, s],
            send_sem=s_sem.at[t - 1, s], recv_sem=r_sem.at[t - 1, s],
            device_id=(y, x, zrel(d), c), device_id_type=MESH,
        )

    def first_half(d):
        return (0, HALF) if d > 0 else (HALF, MOST)

    def has(d, t, s):
        return t > 1 or first_half(d)[0] <= s < first_half(d)[1]

    def qstep(d, t, s, add):
        out, into = (sp, rp) if d > 0 else (sm, rm)
        own = pp[s, c, zrel(d * (top + 1 - t))]
        if add:
            qsend(d, t - 1, s).wait_recv()
            own = (own.astype(F32) + into[t - 2, s].astype(F32)).astype(BF)
        out[t - 1, s] = own
        qsend(d, t, s).start()

    def added(s):
        pair_copy(s).wait_recv()

        @pl.loop(0, nz)
        def _(zz):
            pp[s, c, zz] = (pp[s, c, zz].astype(F32) + rr[s, zz].astype(F32)).astype(BF)

        for d in (1, -1):
            if has(d, 1, s):
                qstep(d, 1, s, False)
            elif top > 1:
                qstep(d, 2, s, False)

    def ysend(d, t, s):
        blk = yb.at[yrel(-d * (t - 1)), s]
        s_sem, r_sem = (ys_p, yr_p) if d > 0 else (ys_m, yr_m)
        return pltpu.make_async_remote_copy(
            src_ref=blk, dst_ref=blk, send_sem=s_sem.at[t - 1, s], recv_sem=r_sem.at[t - 1, s],
            device_id=(yrel(d), x, z, c), device_id_type=MESH,
        )

    def yhas(d, t, s):
        return t < ytop or first_half(d)[0] <= s < first_half(d)[1]

    def yrecv(d, t, s):
        blk = yb.at[yrel(-d * t), s]
        pltpu.make_async_copy(blk, blk, (yr_p if d > 0 else yr_m).at[t - 1, s]).wait()

    def done(s):
        total = pp[s, c, z].astype(F32)
        for d, into in ((1, rp), (-1, rm)):
            if has(d, top, s):
                qsend(d, top, s).wait_recv()
                total = total + into[top - 1, s].astype(F32)
        yb[y, s] = total.astype(BF)
        for d in (1, -1):
            if yhas(d, 1, s):
                ysend(d, 1, s).start()

    def ystep(t, s):
        for d in (1, -1):
            if yhas(d, t, s):
                yrecv(d, t, s)
                if t < ytop and yhas(d, t + 1, s):
                    ysend(d, t + 1, s).start()

    for s in range(MOST + 1):
        if s == 0:
            for zz in before:
                block_in(zz)
        if s < MOST:
            for zz in before:
                block_slot(zz, s)
            partial(s)
        if s:
            added(s - 1)
    for t in range(2, top + 1):
        for s in range(MOST):
            for d in (1, -1):
                if t > 2 or has(d, 1, s):
                    qstep(d, t, s, True)
    for s in range(MOST):
        done(s)
    for t in range(1, ytop + 1):
        for s in range(MOST):
            ystep(t, s)

    def xcopy(i, m):
        to = xrel(i)
        part = pl.ds(m * PAIR_DEV, PAIR_DEV)
        return pltpu.make_async_remote_copy(
            src_ref=xs.at[to, part], dst_ref=(xr_d, xr_m)[m].at[x], send_sem=xs_s.at[m, i], recv_sem=xs_r.at[m, i],
            device_id=(y, to, z, c), device_id_type=MESH,
        )

    for m in (1, 0):
        for i in list(range(1, nx)) + [0]:
            to = xrel(i)
            for j in range(m * PAIR_DEV, (m + 1) * PAIR_DEV):
                got = yb[loc_t[to * 4 + j], loc_t[4 * nx + to * 4 + j]]
                if i:
                    xs[to, j] = got
                else:
                    (xr_d, xr_m)[m][to, j - m * PAIR_DEV] = got
            if i:
                xcopy(i, m).start()

    for f in fetch[3:]:
        f.wait()
    for i in range(1, nx):
        xcopy(i, 1).wait_recv()

    srows = mask_d.shape[0]
    at_r = lax.broadcasted_iota(jnp.int32, (srows, 128), 0)
    at_l = lax.broadcasted_iota(jnp.int32, (srows, 128), 1)

    def ordered(m, j, spread, mask):
        base = (xr_d, xr_m)[m][loc_t[8 * nx + x * 4 + m * PAIR_DEV + j], j].astype(F32)
        last = jnp.zeros((NB, 128), F32)
        lane = lax.broadcasted_iota(jnp.int32, (NB, 128), 1)
        for k in range(CG):
            moved = pltpu.roll(base[k * NB:(k + 1) * NB, :], 128 - (WIDE - k * TAIL), 1)
            last = jnp.where((lane >= k * TAIL) & (lane < (k + 1) * TAIL), moved, last)
        got = jnp.concatenate([base, last, jnp.zeros((srows - units * NB, 128), F32)], axis=0)
        kept = [
            jnp.where((at_r < units * NB) & (at_l >= k * NB) & (at_l < (k + 1) * NB), got, 0.0).astype(BF)
            for k in range(CW)
        ]
        parts = []
        for k in range(CW):
            wide = jnp.dot(kept[k], spread[...], preferred_element_type=F32)
            parts.append((wide * mask[...].astype(F32)).astype(BF))
        return jnp.dot(collect[...], jnp.concatenate(parts, axis=0), preferred_element_type=F32)

    rpad = up(share, 32)
    turned = jnp.concatenate(
        [ordered(1, j, spread_m, mask_m) for j in range(PAIR_DEV)]
        + [jnp.zeros((128 - PAIR_DEV * rpad, rows * rpad), F32)], axis=0,
    ).T.astype(BF)
    for r in range(rows):
        ms[r] = turned[r * rpad:(r + 1) * rpad, :]
    mr[row] = ms[row]

    def mcopy(i):
        to = lax.rem(row + i, rows)
        return pltpu.make_async_remote_copy(
            src_ref=ms.at[to], dst_ref=mr.at[row], send_sem=ms_s.at[i], recv_sem=ms_r.at[i],
            device_id=at_row(to), device_id_type=MESH,
        )

    @pl.loop(1, rows)
    def _(i):
        mcopy(i).start()

    for i in range(1, nx):
        xcopy(i, 0).wait_recv()
    out_d[...] = jnp.stack(
        [ordered(0, j, spread_d, mask_d)[:share, :NB * NB] for j in range(PAIR_DEV)], axis=1
    ).astype(BF)

    @pl.loop(1, rows)
    def _(i):
        mcopy(i).wait_recv()

    out_m[...] = jnp.stack([
        jnp.concatenate(
            [mr[r].astype(F32)[:share, j * rpad:j * rpad + share] for r in range(rows)], axis=1
        ) for j in range(PAIR_DEV)
    ], axis=1).astype(BF)

    for n in range(2):
        for i in range(ny):
            if i:
                by(n, i).wait_send()
            for k in range(1, nx):
                bx(n, i, k).wait_send()
    for t in range(1, top + 1):
        for h in range(CHUNKS):
            for d in (1, -1):
                if g_has(d, t, h):
                    gsend(d, t, h).wait_send()
    for k in range(nz):
        for h in range(2):
            sibling(k, c, h).wait_send()
    for s in range(MOST):
        pair_copy(s).wait_send()
        for t in range(1, top + 1):
            for d in (1, -1):
                if has(d, t, s):
                    qsend(d, t, s).wait_send()
        for t in range(1, ytop + 1):
            for d in (1, -1):
                if yhas(d, t, s):
                    ysend(d, t, s).wait_send()
    for m in range(2):
        for i in range(1, nx):
            xcopy(i, m).wait_send()

    @pl.loop(1, rows)
    def _(i):
        mcopy(i).wait_send()


def constants(rows):
    share = NB * NB // rows
    units = NB * CG // rows
    srows = up(units * NB, 16)
    rpad = up(share, 32)
    lane = np.arange(128)
    plain = np.arange(up(NB * NB, 128))
    wd = np.where(plain < NB * NB, plain, -1)
    padded = np.arange(rows * rpad)
    wdm = np.where(padded % rpad < share, padded // rpad * share + padded % rpad, -1)
    r = np.arange(srows)

    def two(cols):
        spread = (lane[:, None] < CW * NB) & (cols[None, :] >= 0) & (lane[:, None] % NB == cols[None, :] % NB)
        mask = (r[:, None] < units * NB) & (cols[None, :] >= 0) & (r[:, None] % NB == cols[None, :] // NB)
        return spread, mask

    k = np.arange(CW * srows)
    out = np.arange(rpad)
    rr = k % srows
    collect = (
        (rr[None, :] < units * NB) & (out[:, None] < share)
        & (rr[None, :] // NB == out[:, None] // CW) & (k[None, :] // srows == out[:, None] % CW)
    )
    return [a.astype(np.float32).astype(BF) for a in (*two(wd), *two(wdm), collect)]


def solution(mesh):
    sizes = tuple(int(np.prod([mesh.shape[a]])) for a in ("pb", "row"))
    nx, ny, nz = GRID.get(sizes, (4, 8, 8))
    split = Mesh(mesh.devices.reshape(ny, nx, nz, 2), ("y", "x", "z", "c"))
    npb, rows = ny * nx, 2 * nz
    share, units = NB * NB // rows, NB * CG // rows
    srows, rpad = up(units * NB, 16), up(share, 32)
    top, ytop = nz // 2, ny // 2
    dma = pltpu.SemaphoreType.DMA

    def shards(val, con, screened, pair_list, transfer_index, owner_map):
        pairs = pair_list.shape[0]
        consts = [jnp.asarray(a) for a in constants(rows)]
        vmem, anywhere = pl.BlockSpec(memory_space=pltpu.VMEM), pl.BlockSpec(memory_space=pl.ANY)
        points = screened.shape[2]
        blk = ((units - 1) * NB, 128)
        scratch = [
            pltpu.VMEM(val.shape, BF), pltpu.VMEM(con.shape, BF),
            pltpu.VMEM((256, points), BF),
            *[pltpu.VMEM(a.shape, BF) for a in consts],
            pltpu.VMEM((ny, nx, KB, 128), BF),
            pltpu.VMEM((ny, nx, KB, 128), BF),
            pltpu.VMEM((rows, 2 * MOST, KB, 128), BF),
            pltpu.VMEM((MOST, NB * BP, 256), F32),
            pltpu.VMEM((NB * BP, 512), BF),
            pltpu.VMEM((NB * BP, 256), BF),
            pltpu.VMEM((rows, *blk), F32),
            pltpu.VMEM((MOST, 2, nz, *blk), BF),
            pltpu.VMEM((MOST, nz, *blk), BF),
            *[pltpu.VMEM((top, MOST, *blk), BF) for _ in range(4)],
            pltpu.VMEM((ny, MOST, *blk), BF),
            pltpu.VMEM((nx, 2 * PAIR_DEV, *blk), BF),
            pltpu.VMEM((nx, PAIR_DEV, *blk), BF),
            pltpu.VMEM((nx, PAIR_DEV, *blk), BF),
            pltpu.VMEM((rows, rpad, 128), BF),
            pltpu.VMEM((rows, rpad, 128), BF),
            pltpu.SMEM((12 * nx,), jnp.int32),
            dma((8,)),
            dma((2, ny)), dma((2, ny)), dma((2, ny, nx)), dma((2, ny, nx)),
            *[dma((top, CHUNKS)) for _ in range(4)],
            dma((nz, 2)), dma((nz, 2)),
            dma((MOST,)), dma((MOST,)),
            *[dma((top, MOST)) for _ in range(4)],
            *[dma((ytop, MOST)) for _ in range(4)],
            dma((2, nx)), dma((2, nx)), dma((rows,)), dma((rows,)),
        ]
        result = jax.ShapeDtypeStruct((share, PAIR_DEV, NB * NB), BF)
        direct, mirror = pl.pallas_call(
            functools.partial(kernel, ny, nx, nz, pairs),
            out_shape=(result, result),
            in_specs=[*[pl.BlockSpec(memory_space=pltpu.SMEM)] * 3, *[anywhere] * 8],
            out_specs=(vmem, vmem),
            scratch_shapes=scratch,
            compiler_params=pltpu.CompilerParams(
                collective_id=0, has_side_effects=True, vmem_limit_bytes=60 * 2**20
            ),
        )(transfer_index.T, pair_list.T, owner_map, val, con, screened, *consts)
        return direct.transpose(1, 0, 2), mirror.transpose(1, 0, 2)

    in_specs = (P(("y", "x"), None, ("z", "c")), P(("y", "x"), None, ("z", "c")),
                P(("y", "x"), ("z", "c"), None), P(), P(), P())
    out = P(("y", "x"), ("z", "c"), None)
    return jax.shard_map(shards, mesh=split, in_specs=in_specs, out_specs=(out, out), check_vma=False)


GRID = {(4, 4): (2, 2, 2), (2, 8): (1, 2, 4)}
```
